512 devices in a mesh: task: 8 (over y_lo, x), ctx: 64 (over y_hi, z, core).
Axes of the slice: x: 4, y: 8 (y_hi: 4, y_lo: 2; y = y_hi * 2 + y_lo), z: 8, core: 2. Of those that a mesh axis runs over, the one named last changes fastest.
Arguments:
- base_queries: bfloat16 [8, 8192, 2048], P('task', 'ctx'), may hold values from -48 to 48
- adapter_input: bfloat16 [8, 8192, 16], P('task', 'ctx'), may hold values from -6 to 6
- adapter_up_weight: bfloat16 [8, 16, 2048], P('task'), may hold values from -1.5 to 1.5
- projected_keys: bfloat16 [8, 8192, 512], P('task', 'ctx'), may hold values from -6 to 6
- projected_values: bfloat16 [8, 8192, 512], P('task', 'ctx'), may hold values from -6 to 6
- output_gradient: bfloat16 [8, 8192, 2048], P('task', 'ctx'), may hold values from -0.52734375 to 0.52734375
- segments: int32 [8, 8192], P('task', 'ctx'), may hold values from 0 to 20, never falling along the last dimension, each value on 1 to 768 neighbouring positions
- solution: float32 [8, 32768], P('task'), may hold values from -1.5 to 1.5
- residual: float32 [8, 32768], P('task'), may hold values from -1.5 to 1.5
- direction: float32 [8, 32768], P('task'), may hold values from -1.5 to 1.5
- damping: float32 [8], P('task'), may hold values from 2 to 8
Outputs:
- new_solution: float32 [8, 32768], P('task', 'ctx')
- new_residual: float32 [8, 32768], P('task', 'ctx')
- new_direction: float32 [8, 32768], P('task', 'ctx')
- meta_gradient: float32 [32768], P('ctx')
The draws below stay inside these ranges and needn't reach their ends.
Inputs may be any that keep to these rules, and one draw needn't show every extreme that they name: `segments`: segment numbers never fall along a task's tokens; each document holds 1 to 768 tokens, and some document holds exactly 768.
All inputs are finite; a program needn't handle non-finite values.
Results may differ from the reference program's by a relative error of at most 0.0073.
Values may be sent and summed in bfloat16 or wider, within the bound.
No kernel may reach another device: no remote copies, remote signals or barrier semaphores. Data moves between devices by JAX's collectives and lax.ppermute only.
A program may use at most 64 MiB of HBM per device.

```python
import math
import jax
import jax.numpy as jnp
import numpy as np
from jax import lax

HEADS = 16
KV_HEADS = 4
HEAD_DIM = 128
ADAPTER_RANK = 16
TOKENS_PER_SHARD = 128
TASK_COUNT = 8
TASK_TOKENS = 8192
DOC = 768
DOCS = 21
QUERY_FEATURES = 2048
KW = 512
PARAMS = 32768


def joint_draw(key):
    seeded = jax.random.fold_in(key, 7301)
    query_key, key_key = jax.random.split(seeded, 2)
    key_field = jnp.clip(jax.random.normal(key_key, (TASK_COUNT, TASK_TOKENS, KV_HEADS, HEAD_DIM), jnp.float32), -6.0, 6.0)
    query_field = jnp.clip(jax.random.normal(query_key, (TASK_COUNT, TASK_TOKENS, HEADS, HEAD_DIM), jnp.float32), -6.0, 6.0)
    return (query_field.reshape(TASK_COUNT, TASK_TOKENS, HEADS * HEAD_DIM), key_field.reshape(TASK_COUNT, TASK_TOKENS, KV_HEADS * HEAD_DIM))


def draw_base_queries(key, part):
    return joint_draw(key)[0].astype(jnp.bfloat16)


def draw_projected_keys(key, part):
    return joint_draw(key)[1].astype(jnp.bfloat16)


def level_of(key, dims, shards, low, high):
    factor_of = 1.0
    for axis_at, blocks in shards:
        heights = jax.random.uniform(jax.random.fold_in(jax.random.fold_in(key, 6), axis_at), (blocks,), jnp.float32, low / len(shards), high / len(shards))
        factor_of = factor_of * jnp.repeat(jnp.exp(heights), dims[axis_at] // blocks).reshape((-1,) + (1,) * (len(dims) - 1 - axis_at))
    return factor_of


def length_profile(number_of, total, limit, lean):
    weights = [(1 << 20) // math.isqrt(standing ** lean) + 1 for standing in range(2, number_of + 1)]
    spare, counts = total - limit - (number_of - 1), [1] * (number_of - 1)
    while spare > 0:
        free = [i for i in range(number_of - 1) if counts[i] < limit]
        mass, left = sum([weights[i] for i in free]), spare
        for i in free:
            more = min(limit - counts[i], max(1, left * weights[i] // mass), spare)
            counts[i] = counts[i] + more
            spare = spare - more
    return np.array([limit] + counts)


def ragged(stream_key, amount, total, bound, slope):
    if amount == 2:
        one = jax.random.randint(stream_key, (), max(1, total - bound), min(bound, total - 1) + 1)
        return jnp.stack([one, total - one])
    lengths = jnp.asarray(length_profile(amount, total, bound, slope), jnp.int32)
    pairs = (amount - 1) // 2
    donor, sink = lengths[1:1 + 2 * pairs:2], lengths[2:2 + 2 * pairs:2]
    room = jnp.minimum(donor - 1, bound - sink)
    shifted = jax.random.randint(jax.random.fold_in(stream_key, 1), (pairs,), 0, 1 << 20) % (room + 1)
    lengths = lengths.at[1:1 + 2 * pairs:2].set(donor - shifted).at[2:2 + 2 * pairs:2].set(sink + shifted)
    return lengths[jax.random.permutation(jax.random.fold_in(stream_key, 2), amount)]


def bell_draw(stream_key, dims, spread, limit, cuts=(), kind=jnp.bfloat16):
    array = jax.random.normal(stream_key, dims, jnp.float32) * spread
    if len(cuts) > 0:
        array = level_of(stream_key, dims, cuts, -0.22, 0.18) * array
    return jnp.clip(array, min=-limit, max=limit).astype(kind)


def setup_inputs(seed: int = 0) -> dict:
    arg_keys = jax.random.split(jax.random.key(seed), 12)
    base_queries = draw_base_queries(jax.random.fold_in(arg_keys[11], 71), 0)
    adapter_input = bell_draw(arg_keys[1], (TASK_COUNT, TASK_TOKENS, ADAPTER_RANK), 1.0, 6.0, ((0, 8), (1, 64)))
    adapter_up_weight = bell_draw(arg_keys[2], (TASK_COUNT, ADAPTER_RANK, QUERY_FEATURES), ADAPTER_RANK ** -0.5, 1.5, ((0, 8),))
    projected_keys = draw_projected_keys(jax.random.fold_in(arg_keys[11], 71), 0)
    projected_values = bell_draw(arg_keys[4], (TASK_COUNT, TASK_TOKENS, KW), 1.0, 6.0, ((0, 8), (1, 64)))
    output_gradient = bell_draw(arg_keys[5], (TASK_COUNT, TASK_TOKENS, QUERY_FEATURES), (HEAD_DIM ** -0.5), 0.52734375, ((0, 8), (1, 64)))
    segments = jax.vmap(lambda own: jnp.searchsorted(jnp.cumsum(ragged(own, DOCS, TASK_TOKENS, DOC, 0)), jnp.arange(TASK_TOKENS), side="right"))(jax.random.split(arg_keys[6], TASK_COUNT)).reshape((TASK_COUNT, TASK_TOKENS)).astype(jnp.int32)
    solution = bell_draw(arg_keys[7], (TASK_COUNT, PARAMS), 0.25, 1.5, ((0, 8),), jnp.float32)
    residual = bell_draw(arg_keys[8], (TASK_COUNT, PARAMS), 0.25, 1.5, ((0, 8),), jnp.float32)
    direction = bell_draw(arg_keys[9], (TASK_COUNT, PARAMS), 0.25, 1.5, ((0, 8),), jnp.float32)
    damping = jnp.clip(jnp.exp(math.log(8.0) - 1.3862944 * jax.random.uniform(arg_keys[10], (TASK_COUNT,), jnp.float32) ** level_of(arg_keys[10], (TASK_COUNT,), ((0, 8),), -0.2, 0.2)), 2.0, 8.0)
    return dict(base_queries=base_queries, adapter_input=adapter_input, adapter_up_weight=adapter_up_weight, projected_keys=projected_keys, projected_values=projected_values, output_gradient=output_gradient, segments=segments, solution=solution, residual=residual, direction=direction, damping=damping)


def attend(query_matrix, tangent_vectors, grads_in, key_window, value_window, allowed):
    per_group = HEADS // KV_HEADS
    score_scale = HEAD_DIM ** -0.5
    row_count = query_matrix.shape[0]
    head_parts = []
    for kv_index in range(KV_HEADS):
        low_col = kv_index * per_group * HEAD_DIM
        high_col = low_col + per_group * HEAD_DIM
        query_head = query_matrix[:, low_col:high_col].reshape(row_count, per_group, HEAD_DIM).astype(jnp.float32)
        tangent_head = tangent_vectors[:, low_col:high_col].reshape(row_count, per_group, HEAD_DIM).astype(jnp.float32)
        grad_head = grads_in[:, low_col:high_col].reshape(row_count, per_group, HEAD_DIM).astype(jnp.float32)
        key_head = key_window[:, kv_index * HEAD_DIM:(kv_index + 1) * HEAD_DIM].astype(jnp.float32)
        value_head = value_window[:, kv_index * HEAD_DIM:(kv_index + 1) * HEAD_DIM].astype(jnp.float32)
        scores = jnp.einsum("tgd,kd->tgk", query_head, key_head) * score_scale
        slopes = jnp.einsum("tgd,kd->tgk", tangent_head, key_head) * score_scale
        pulls = jnp.einsum("tgd,kd->tgk", grad_head, value_head)
        key_mask = allowed[:, None, :]
        masked = jnp.where(key_mask, scores, -1e30)
        row_max = jnp.max(masked, axis=2, keepdims=True)
        exp_terms = jnp.exp(masked - row_max)
        probability = exp_terms / jnp.sum(exp_terms, axis=2, keepdims=True)
        mean_slope = jnp.sum(probability * slopes, axis=2, keepdims=True)
        mean_pull = jnp.sum(probability * pulls, axis=2, keepdims=True)
        centred = (slopes - mean_slope) * (pulls - mean_pull)
        covariance = jnp.sum(probability * centred, axis=2, keepdims=True)
        coef_rounded = (probability * (centred - covariance)).astype(jnp.bfloat16)
        coef_back = lax.optimization_barrier(coef_rounded).astype(jnp.float32)
        head_rows = jnp.einsum("tgk,kd->tgd", coef_back, key_head) * score_scale
        head_parts.append(head_rows.reshape(row_count, per_group * HEAD_DIM))
    return jnp.concatenate(head_parts, axis=1)


def task_contribution(base_queries, adapter_input, adapter_up_weight, projected_keys, projected_values, output_gradient, segments, direction):
    query_matrix = (base_queries.astype(jnp.float32) + jnp.dot(adapter_input, adapter_up_weight, preferred_element_type=jnp.float32)).astype(jnp.bfloat16)
    shift_matrix_fn = direction.reshape(ADAPTER_RANK, HEADS * HEAD_DIM)
    tangent_vectors = jnp.dot(adapter_input.astype(jnp.float32), shift_matrix_fn, precision=lax.Precision.HIGHEST).astype(jnp.bfloat16)
    key_width = KV_HEADS * HEAD_DIM
    key_padded = jnp.concatenate([jnp.zeros((DOC, key_width), jnp.bfloat16), projected_keys], axis=0)
    value_padded = jnp.concatenate([jnp.zeros((DOC, key_width), jnp.bfloat16), projected_values], axis=0)
    seg_padded = jnp.concatenate([jnp.zeros((DOC,), jnp.int32), segments.astype(jnp.int32)], axis=0)
    window = DOC + TOKENS_PER_SHARD

    def one_block(block_id):
        leading_row = (block_id * TOKENS_PER_SHARD).astype(jnp.int32)
        query_rows = lax.dynamic_slice_in_dim(query_matrix, leading_row, TOKENS_PER_SHARD, 0)
        tangent_rows = lax.dynamic_slice_in_dim(tangent_vectors, leading_row, TOKENS_PER_SHARD, 0)
        grad_rows = lax.dynamic_slice_in_dim(output_gradient, leading_row, TOKENS_PER_SHARD, 0)
        adapter_rows = lax.dynamic_slice_in_dim(adapter_input, leading_row, TOKENS_PER_SHARD, 0)
        seg_rows = lax.dynamic_slice_in_dim(segments.astype(jnp.int32), leading_row, TOKENS_PER_SHARD, 0)
        key_window = lax.dynamic_slice_in_dim(key_padded, leading_row, window, 0)
        value_window = lax.dynamic_slice_in_dim(value_padded, leading_row, window, 0)
        seg_window = lax.dynamic_slice_in_dim(seg_padded, leading_row, window, 0)
        key_place = leading_row - DOC + jnp.arange(window, dtype=jnp.int32)
        query_place = leading_row + jnp.arange(TOKENS_PER_SHARD, dtype=jnp.int32)
        allowed = (key_place[None, :] <= query_place[:, None]) & (key_place[None, :] >= 0) & (seg_window[None, :] == seg_rows[:, None])
        curvature_product_rows = attend(query_rows, tangent_rows, grad_rows, key_window, value_window, allowed).astype(jnp.bfloat16)
        return jnp.dot(adapter_rows.T, curvature_product_rows, preferred_element_type=jnp.float32)

    block_terms = lax.map(one_block, jnp.arange(TASK_TOKENS // TOKENS_PER_SHARD, dtype=jnp.int32))
    return jnp.sum(block_terms, axis=0).reshape(ADAPTER_RANK * HEADS * HEAD_DIM)


def reference(base_queries, adapter_input, adapter_up_weight, projected_keys, projected_values, output_gradient, segments, solution, residual, direction, damping):
    def task_wise(items):
        return task_contribution(items[0], items[1], items[2], items[3], items[4], items[5], items[6], items[7])

    complete_curvature_product = lax.map(task_wise, (base_queries, adapter_input, adapter_up_weight, projected_keys, projected_values, output_gradient, segments, direction))
    curved = direction + complete_curvature_product / damping[:, None]
    old_norm = jnp.sum(residual * residual, axis=1)
    step_len = old_norm / jnp.sum(direction * curved, axis=1)
    new_solution = solution + step_len[:, None] * direction
    new_residual = residual - step_len[:, None] * curved
    ratio = jnp.sum(new_residual * new_residual, axis=1) / old_norm
    new_direction = new_residual + ratio[:, None] * direction
    meta_gradient = jnp.mean(new_solution, axis=0)
    return new_solution, new_residual, new_direction, meta_gradient
```

```python
import math

import jax
import jax.numpy as jnp
from jax import lax
from jax.experimental import pallas as pl
from jax.experimental.pallas import tpu as pltpu
from jax.sharding import Mesh
from jax.sharding import PartitionSpec as P

HEAD_DIM = 128
RANK = 16
BLOCK = 128
CHUNK = 2 * BLOCK
SPAN = 3
WINDOW = 7 * BLOCK
GROUPS = 2
PER_GROUP = 4
HALF = GROUPS * PER_GROUP * HEAD_DIM
KHALF = GROUPS * HEAD_DIM
GFEAT = PER_GROUP * HEAD_DIM
SEG_ROWS = 16
F32 = jnp.float32
BF16 = jnp.bfloat16
CTX = ("yh", "z", "core")
NT = (((1,), (1,)), ((), ()))
NN = (((1,), (0,)), ((), ()))


def dot(a, b, dims=NN):
    return lax.dot_general(a, b, dims, preferred_element_type=F32)


def fold(x):
    return x.reshape(x.shape[0] // 8, 8, x.shape[1])


def attend_kernel(
    qg, c0, c1, c2, c3, up, dmat, rmat, out, keys, keys_t, vals, bias, qs, ts, at, s_ref, t_ref, u_ref, c_ref
):
    chunks = (c0, c1, c2, c3)
    a_pad = qg[:, 2 * HALF : 2 * HALF + 128]
    a = a_pad[:, :RANK]
    qs[...] = (qg[:, :HALF].astype(F32) + dot(a, up[...])).astype(BF16)
    d = dmat[...]
    d1 = d.astype(BF16)
    rest = d - d1.astype(F32)
    d2 = rest.astype(BF16)
    d3 = (rest - d2.astype(F32)).astype(BF16)
    ts[...] = (dot(a, d1) + dot(a, d2) + dot(a, d3)).astype(BF16)
    at[...] = jnp.transpose(a_pad.astype(F32))[:RANK].astype(BF16)
    for j, c in enumerate(chunks):
        rows = slice(j * CHUNK, (j + 1) * CHUNK)
        for g in range(GROUPS):
            k = c[:CHUNK, g * HEAD_DIM : (g + 1) * HEAD_DIM]
            keys[g, rows, :] = k
            keys_t[g, :, rows] = jnp.transpose(k.astype(F32)).astype(BF16)
            vals[g, rows, :] = c[:CHUNK, KHALF + g * HEAD_DIM : KHALF + (g + 1) * HEAD_DIM]
    seg_rows = [c[CHUNK : CHUNK + SEG_ROWS, :CHUNK].astype(F32)[0:1] for c in chunks]
    tri = lax.broadcasted_iota(jnp.int32, (BLOCK, BLOCK), 0) <= lax.broadcasted_iota(jnp.int32, (BLOCK, BLOCK), 1)
    key_seg = []
    for kb in range(8):
        row = seg_rows[kb // 2][:, (kb % 2) * BLOCK : (kb % 2 + 1) * BLOCK]
        key_seg.append(jnp.transpose(jnp.broadcast_to(row, (BLOCK, BLOCK))))
    for b in range(2):
        query_seg = jnp.broadcast_to(seg_rows[3][:, b * BLOCK : (b + 1) * BLOCK], (BLOCK, BLOCK))
        for w in range(7):
            ok = key_seg[w + b] == query_seg
            if w == 6:
                ok = ok & tri
            bias[b, w * BLOCK : (w + 1) * BLOCK, :] = jnp.where(ok, 0.0, -1e30)
    out[...] = jnp.zeros_like(out)
    cexp = HEAD_DIM**-0.5 * math.log2(math.e)

    def step(i, carry):
        g, b = i // 2, i % 2
        off = pl.multiple_of(b * BLOCK, BLOCK)
        kw = keys[g, pl.ds(off, WINDOW), :]
        vw = vals[g, pl.ds(off, WINDOW), :]
        ktw = keys_t[g, :, pl.ds(off, WINDOW)]
        for pair in range(2):

            def two(ref, base):
                parts = []
                for e in range(2):
                    col = pl.multiple_of(base + g * GFEAT + (pair * 2 + e) * HEAD_DIM, HEAD_DIM)
                    parts.append(ref[pl.ds(off, BLOCK), pl.ds(col, HEAD_DIM)])
                return jnp.concatenate(parts, axis=0)

            s_ref[pair] = dot(kw, two(qs, 0), NT)
            t_ref[pair] = dot(kw, two(ts, 0), NT)
            u_ref[pair] = dot(vw, two(qg, HALF), NT)
        for pair in range(2):
            scales = []
            for e in range(2):
                lanes = slice(e * BLOCK, (e + 1) * BLOCK)
                m8 = jnp.full((8, BLOCK), -3e38, F32)
                for w in range(7):
                    rows = slice(w * BLOCK, (w + 1) * BLOCK)
                    m8 = jnp.maximum(m8, jnp.max(fold(s_ref[pair, rows, lanes] + bias[b, rows, :]), axis=0))
                m = jnp.max(m8, axis=0, keepdims=True)
                z8 = et8 = eu8 = etu8 = jnp.zeros((8, BLOCK), F32)
                for w in range(7):
                    rows = slice(w * BLOCK, (w + 1) * BLOCK)
                    ex = jnp.exp2((s_ref[pair, rows, lanes] + bias[b, rows, :] - m) * cexp)
                    s_ref[pair, rows, lanes] = ex
                    et = ex * t_ref[pair, rows, lanes]
                    u = u_ref[pair, rows, lanes]
                    z8 = z8 + jnp.sum(fold(ex), axis=0)
                    et8 = et8 + jnp.sum(fold(et), axis=0)
                    eu8 = eu8 + jnp.sum(fold(ex * u), axis=0)
                    etu8 = etu8 + jnp.sum(fold(et * u), axis=0)
                inv = 1.0 / jnp.sum(z8, axis=0, keepdims=True)
                mt = jnp.sum(et8, axis=0, keepdims=True) * inv
                mu = jnp.sum(eu8, axis=0, keepdims=True) * inv
                cov = jnp.sum(etu8, axis=0, keepdims=True) * inv - mt * mu
                for w in range(7):
                    rows = slice(w * BLOCK, (w + 1) * BLOCK)
                    coef = s_ref[pair, rows, lanes] * (
                        (t_ref[pair, rows, lanes] - mt) * (u_ref[pair, rows, lanes] - mu) - cov
                    )
                    c_ref[pair, rows, lanes] = coef.astype(BF16)
                scales.append(inv * (1.0 / HEAD_DIM))
            hv = dot(ktw, c_ref[pair])
            ab = at[:, pl.ds(off, BLOCK)]
            for e in range(2):
                lanes = slice(e * BLOCK, (e + 1) * BLOCK)
                head = (hv[:, lanes] * scales[e]).astype(BF16)
                cols = slice((pair * 2 + e) * HEAD_DIM, (pair * 2 + e + 1) * HEAD_DIM)
                out[g, :, cols] += dot(ab, head, NT)
        return carry

    lax.fori_loop(0, 4, step, 0)
    dh = rh = jnp.zeros((1, 1), F32)
    for g in range(GROUPS):
        h = out[g, :, :GFEAT]
        cols = slice(g * GFEAT, (g + 1) * GFEAT)
        dh = dh + jnp.sum(h * d[:, cols], keepdims=True)
        rh = rh + jnp.sum(h * rmat[:, cols], keepdims=True)
    lane = lax.broadcasted_iota(jnp.int32, (RANK, 128), 1)
    tail = jnp.where(lane == 0, dh, jnp.where(lane == 1, rh, 0.0))
    for g in range(GROUPS):
        out[g, :, GFEAT:] = tail


def attend(qg, chunks, up, dmat, rmat):
    vm = pltpu.VMEM
    return pl.pallas_call(
        attend_kernel,
        out_shape=jax.ShapeDtypeStruct((GROUPS, RANK, GFEAT + 128), F32),
        in_specs=[pl.BlockSpec(memory_space=vm)] * 8,
        out_specs=pl.BlockSpec(memory_space=vm),
        scratch_shapes=[
            vm((GROUPS, 4 * CHUNK, HEAD_DIM), BF16),
            vm((GROUPS, HEAD_DIM, 4 * CHUNK), BF16),
            vm((GROUPS, 4 * CHUNK, HEAD_DIM), BF16),
            vm((2, WINDOW, BLOCK), F32),
            vm((CHUNK, HALF), BF16),
            vm((CHUNK, HALF), BF16),
            vm((RANK, CHUNK), BF16),
            vm((2, WINDOW, CHUNK), F32),
            vm((2, WINDOW, CHUNK), F32),
            vm((2, WINDOW, CHUNK), F32),
            vm((2, WINDOW, CHUNK), BF16),
        ],
        compiler_params=pltpu.CompilerParams(vmem_limit_bytes=32 * 1024 * 1024),
        cost_estimate=pl.CostEstimate(flops=2_000_000_000, bytes_accessed=4_000_000, transcendentals=2_000_000),
        name="attend",
    )(qg, *chunks, up, dmat, rmat)


def per_core(x):
    rows, _, _, n = x.shape
    return x.transpose(2, 0, 1, 3).reshape(2, rows, 2 * n)


def per_device(
    base_queries, adapter_input, adapter_up_weight, projected_keys, projected_values, output_gradient,
    segments, solution, residual, direction, damping,
):
    core = lax.axis_index("core")
    n_yh, n_z = lax.axis_size("yh"), lax.axis_size("z")
    ctx_size = n_yh * n_z * 2
    idx = lax.axis_index(CTX)

    keys = per_core(projected_keys[0].reshape(BLOCK, 2, 2, HEAD_DIM))
    values = per_core(projected_values[0].reshape(BLOCK, 2, 2, HEAD_DIM))
    seg = (segments[0] + 1).astype(BF16)
    seg_row = jnp.zeros((SEG_ROWS, 2 * KHALF), BF16).at[0, :BLOCK].set(seg)
    kv = jnp.concatenate([keys, values], axis=2)
    kv = jnp.concatenate([kv, jnp.broadcast_to(seg_row[None], (2, SEG_ROWS, 2 * KHALF))], axis=1)
    kv = lax.all_to_all(kv, "core", 0, 0, tiled=True)
    segs = jnp.concatenate([kv[0, BLOCK:, :BLOCK], kv[1, BLOCK:, :BLOCK], jnp.zeros((SEG_ROWS, 2 * KHALF - CHUNK), BF16)], axis=1)
    own = jnp.concatenate([kv[0, :BLOCK], kv[1, :BLOCK], segs], axis=0)

    pad = jnp.pad(adapter_input[0], ((0, 0), (0, 128 - RANK)))
    qg = jnp.concatenate(
        [
            per_core(base_queries[0].reshape(BLOCK, 2, 2, GFEAT)),
            per_core(output_gradient[0].reshape(BLOCK, 2, 2, GFEAT)),
            jnp.broadcast_to(pad[None], (2, BLOCK, 128)),
        ],
        axis=2,
    )
    qg = lax.all_to_all(qg, "core", 0, 0, tiled=True).reshape(CHUNK, 2 * HALF + 128)

    earlier = []
    for k in range(1, SPAN + 1):
        earlier.append(lax.ppermute(own, CTX, [(s, s + 2 * k) for s in range(ctx_size - 2 * k)]))
    chunks = earlier[::-1] + [own]

    def core_part(x):
        x = x.reshape(RANK, 2, 2, GFEAT)
        return lax.dynamic_index_in_dim(x, core, 2, keepdims=False).reshape(RANK, HALF)

    terms = attend(qg, chunks, core_part(adapter_up_weight[0]), core_part(direction[0]), core_part(residual[0]))

    peers = n_yh * n_z
    terms = terms.transpose(1, 0, 2).reshape(peers, GFEAT + 128)
    got = jnp.sum(lax.all_to_all(terms, ("yh", "z"), 0, 0, tiled=True), axis=0)
    h = got[:GFEAT]
    dh, rh = got[GFEAT], got[GFEAT + 1]
    both = lax.psum(jnp.stack([dh, rh]), "core")
    dh, rh = both[0], both[1]
    hh_part = jnp.sum(h * h)
    hh = jnp.sum(lax.all_to_all(jnp.full((ctx_size, 128), hh_part), CTX, 0, 0, tiled=True)[:, 0])

    damp = damping[0]
    d_full, r_full = direction[0], residual[0]
    old_norm = jnp.sum(r_full * r_full)
    dd = jnp.sum(d_full * d_full)
    rd = jnp.sum(r_full * d_full)
    step_len = old_norm / (dd + dh / damp)
    size = GFEAT
    d_part = lax.dynamic_slice_in_dim(d_full, idx * size, size, 0)
    r_part = lax.dynamic_slice_in_dim(r_full, idx * size, size, 0)
    s_part = lax.dynamic_slice_in_dim(solution[0], idx * size, size, 0)
    new_solution = s_part + step_len * d_part
    n_task = lax.axis_size("task")
    spread = lax.all_to_all(jnp.broadcast_to(new_solution[None], (n_task, size)), "task", 0, 0, tiled=True)
    meta_gradient = jnp.sum(spread, axis=0) / n_task

    curved = d_part + h / damp
    rc = rd + rh / damp
    cc = dd + 2.0 * dh / damp + hh / (damp * damp)
    new_norm = old_norm - 2.0 * step_len * rc + step_len * step_len * cc
    new_residual = r_part - step_len * curved
    new_direction = new_residual + (new_norm / old_norm) * d_part
    return new_solution[None], new_residual[None], new_direction[None], meta_gradient


def solution(mesh):
    n_task, n_ctx = mesh.devices.shape
    split = Mesh(mesh.devices.reshape(n_task, n_ctx // 16, 8, 2), ("task",) + CTX)
    tokens = P("task", CTX, None)
    whole = P("task", None)
    in_specs = (tokens, tokens, P("task", None, None), tokens, tokens, tokens, P("task", CTX), whole, whole, whole, P("task"))
    out_specs = (P("task", CTX), P("task", CTX), P("task", CTX), P(CTX))
    return jax.shard_map(per_device, mesh=split, in_specs=in_specs, out_specs=out_specs, check_vma=False)
```

```python
import math

import jax
import jax.numpy as jnp
from jax import lax
from jax.experimental import pallas as pl
from jax.experimental.pallas import tpu as pltpu
from jax.sharding import Mesh
from jax.sharding import PartitionSpec as P

HEAD_DIM = 128
RANK = 16
BLOCK = 128
CHUNK = 2 * BLOCK
SPAN = 3
WINDOW = 7 * BLOCK
GROUPS = 2
PER_GROUP = 4
HALF = GROUPS * PER_GROUP * HEAD_DIM
KHALF = GROUPS * HEAD_DIM
GFEAT = PER_GROUP * HEAD_DIM
SEG_ROWS = 16
F32 = jnp.float32
BF16 = jnp.bfloat16
CTX = ("yh", "z", "core")
NT = (((1,), (1,)), ((), ()))
NN = (((1,), (0,)), ((), ()))


def dot(a, b, dims=NN):
    return lax.dot_general(a, b, dims, preferred_element_type=F32)


def fold(x):
    return x.reshape(x.shape[0] // 8, 8, x.shape[1])


def attend_kernel(
    qg, c0, c1, c2, c3, up, dmat, rmat, out, keys, keys_t, vals, bias, qs, ts, at, s_ref, t_ref, u_ref, c_ref
):
    chunks = (c0, c1, c2, c3)
    a_pad = qg[:, 2 * HALF : 2 * HALF + 128]
    a = a_pad[:, :RANK]
    qs[...] = (qg[:, :HALF].astype(F32) + dot(a, up[...])).astype(BF16)
    d = dmat[...]
    d1 = d.astype(BF16)
    rest = d - d1.astype(F32)
    d2 = rest.astype(BF16)
    d3 = (rest - d2.astype(F32)).astype(BF16)
    ts[...] = (dot(a, d1) + dot(a, d2) + dot(a, d3)).astype(BF16)
    at[...] = jnp.transpose(a_pad.astype(F32))[:RANK].astype(BF16)
    for j, c in enumerate(chunks):
        rows = slice(j * CHUNK, (j + 1) * CHUNK)
        for g in range(GROUPS):
            k = c[:CHUNK, g * HEAD_DIM : (g + 1) * HEAD_DIM]
            keys[g, rows, :] = k
            keys_t[g, :, rows] = jnp.transpose(k.astype(F32)).astype(BF16)
            vals[g, rows, :] = c[:CHUNK, KHALF + g * HEAD_DIM : KHALF + (g + 1) * HEAD_DIM]
    seg_rows = [c[CHUNK : CHUNK + SEG_ROWS, :CHUNK].astype(F32)[0:1] for c in chunks]
    tri = lax.broadcasted_iota(jnp.int32, (BLOCK, BLOCK), 0) <= lax.broadcasted_iota(jnp.int32, (BLOCK, BLOCK), 1)
    key_seg = []
    for kb in range(8):
        row = seg_rows[kb // 2][:, (kb % 2) * BLOCK : (kb % 2 + 1) * BLOCK]
        key_seg.append(jnp.transpose(jnp.broadcast_to(row, (BLOCK, BLOCK))))
    for b in range(2):
        query_seg = jnp.broadcast_to(seg_rows[3][:, b * BLOCK : (b + 1) * BLOCK], (BLOCK, BLOCK))
        for w in range(7):
            ok = key_seg[w + b] == query_seg
            if w == 6:
                ok = ok & tri
            bias[b, w * BLOCK : (w + 1) * BLOCK, :] = jnp.where(ok, 0.0, -1e30)
    out[...] = jnp.zeros_like(out)
    cexp = HEAD_DIM**-0.5 * math.log2(math.e)

    def step(i, carry):
        g, b = i // 2, i % 2
        off = pl.multiple_of(b * BLOCK, BLOCK)
        kw = keys[g, pl.ds(off, WINDOW), :]
        vw = vals[g, pl.ds(off, WINDOW), :]
        ktw = keys_t[g, :, pl.ds(off, WINDOW)]
        for pair in range(2):

            def two(ref, base):
                parts = []
                for e in range(2):
                    col = pl.multiple_of(base + g * GFEAT + (pair * 2 + e) * HEAD_DIM, HEAD_DIM)
                    parts.append(ref[pl.ds(off, BLOCK), pl.ds(col, HEAD_DIM)])
                return jnp.concatenate(parts, axis=0)

            s_ref[pair] = dot(kw, two(qs, 0), NT)
            t_ref[pair] = dot(kw, two(ts, 0), NT)
            u_ref[pair] = dot(vw, two(qg, HALF), NT)
        for pair in range(2):
            scales = []
            for e in range(2):
                lanes = slice(e * BLOCK, (e + 1) * BLOCK)
                m8 = jnp.full((8, BLOCK), -3e38, F32)
                for w in range(7):
                    rows = slice(w * BLOCK, (w + 1) * BLOCK)
                    m8 = jnp.maximum(m8, jnp.max(fold(s_ref[pair, rows, lanes] + bias[b, rows, :]), axis=0))
                m = jnp.max(m8, axis=0, keepdims=True)
                z8 = et8 = eu8 = etu8 = jnp.zeros((8, BLOCK), F32)
                for w in range(7):
                    rows = slice(w * BLOCK, (w + 1) * BLOCK)
                    ex = jnp.exp2((s_ref[pair, rows, lanes] + bias[b, rows, :] - m) * cexp)
                    s_ref[pair, rows, lanes] = ex
                    et = ex * t_ref[pair, rows, lanes]
                    u = u_ref[pair, rows, lanes]
                    z8 = z8 + jnp.sum(fold(ex), axis=0)
                    et8 = et8 + jnp.sum(fold(et), axis=0)
                    eu8 = eu8 + jnp.sum(fold(ex * u), axis=0)
                    etu8 = etu8 + jnp.sum(fold(et * u), axis=0)
                inv = 1.0 / jnp.sum(z8, axis=0, keepdims=True)
                mt = jnp.sum(et8, axis=0, keepdims=True) * inv
                mu = jnp.sum(eu8, axis=0, keepdims=True) * inv
                cov = jnp.sum(etu8, axis=0, keepdims=True) * inv - mt * mu
                for w in range(7):
                    rows = slice(w * BLOCK, (w + 1) * BLOCK)
                    coef = s_ref[pair, rows, lanes] * (
                        (t_ref[pair, rows, lanes] - mt) * (u_ref[pair, rows, lanes] - mu) - cov
                    )
                    c_ref[pair, rows, lanes] = coef.astype(BF16)
                scales.append(inv * (1.0 / HEAD_DIM))
            hv = dot(ktw, c_ref[pair])
            ab = at[:, pl.ds(off, BLOCK)]
            for e in range(2):
                lanes = slice(e * BLOCK, (e + 1) * BLOCK)
                head = (hv[:, lanes] * scales[e]).astype(BF16)
                cols = slice((pair * 2 + e) * HEAD_DIM, (pair * 2 + e + 1) * HEAD_DIM)
                out[g, :, cols] += dot(ab, head, NT)
        return carry

    lax.fori_loop(0, 4, step, 0)
    dh = rh = jnp.zeros((1, 1), F32)
    for g in range(GROUPS):
        h = out[g, :, :GFEAT]
        cols = slice(g * GFEAT, (g + 1) * GFEAT)
        dh = dh + jnp.sum(h * d[:, cols], keepdims=True)
        rh = rh + jnp.sum(h * rmat[:, cols], keepdims=True)
    lane = lax.broadcasted_iota(jnp.int32, (RANK, 128), 1)
    tail = jnp.where(lane == 0, dh, jnp.where(lane == 1, rh, 0.0))
    for g in range(GROUPS):
        out[g, :, GFEAT:] = tail


def attend(qg, chunks, up, dmat, rmat):
    vm = pltpu.VMEM
    return pl.pallas_call(
        attend_kernel,
        out_shape=jax.ShapeDtypeStruct((GROUPS, RANK, GFEAT + 128), F32),
        in_specs=[pl.BlockSpec(memory_space=vm)] * 8,
        out_specs=pl.BlockSpec(memory_space=vm),
        scratch_shapes=[
            vm((GROUPS, 4 * CHUNK, HEAD_DIM), BF16),
            vm((GROUPS, HEAD_DIM, 4 * CHUNK), BF16),
            vm((GROUPS, 4 * CHUNK, HEAD_DIM), BF16),
            vm((2, WINDOW, BLOCK), F32),
            vm((CHUNK, HALF), BF16),
            vm((CHUNK, HALF), BF16),
            vm((RANK, CHUNK), BF16),
            vm((2, WINDOW, CHUNK), F32),
            vm((2, WINDOW, CHUNK), F32),
            vm((2, WINDOW, CHUNK), F32),
            vm((2, WINDOW, CHUNK), BF16),
        ],
        compiler_params=pltpu.CompilerParams(vmem_limit_bytes=32 * 1024 * 1024),
        cost_estimate=pl.CostEstimate(flops=2_000_000_000, bytes_accessed=4_000_000, transcendentals=2_000_000),
        name="attend",
    )(qg, *chunks, up, dmat, rmat)


def sum_spread_kernel(got, out):
    total = jnp.sum(got[...], axis=0, keepdims=True)
    out[...] = jnp.broadcast_to(total, out.shape)


def norm_kernel(got, h_out, out):
    total = jnp.sum(got[...], axis=0)
    h = total[:, : h_out.shape[1]]
    h_out[...] = h
    tail = total[:, h_out.shape[1] :]
    lane = lax.broadcasted_iota(jnp.int32, tail.shape, 1)
    share = 2.0 / out.shape[0]
    row = jnp.where(lane == 2, jnp.sum(h * h, keepdims=True), tail * share)
    out[...] = jnp.broadcast_to(row[None], out.shape)


def update_kernel(sizes, got, h_all, dot_in, parts, new_solution, new_residual, new_direction, spread):
    total = jnp.sum(got[...], axis=0)
    lane = lax.broadcasted_iota(jnp.int32, total.shape, 1)

    def pick(row, k):
        return jnp.sum(jnp.where(lane == k, row, 0.0), keepdims=True)

    dh, rh, hh = pick(total, 0), pick(total, 1), pick(total, 2)
    consts = dot_in[...]
    rr, dd, rd, damp = (pick(consts, k) for k in range(4))
    size = new_solution.shape[1]
    h = h_all[:, pl.ds(pl.multiple_of(sizes[0] * size, 128), size)]
    sol, res, dirn = parts[0:1], parts[1:2], parts[2:3]
    step_len = rr / (dd + dh / damp)
    curved = dirn + h / damp
    rc = rd + rh / damp
    cc = dd + 2.0 * dh / damp + hh / (damp * damp)
    new_norm = rr - 2.0 * step_len * rc + step_len * step_len * cc
    ns = sol + step_len * dirn
    nr = res - step_len * curved
    new_solution[...] = ns
    new_residual[...] = nr
    new_direction[...] = nr + (new_norm / rr) * dirn
    spread[...] = jnp.broadcast_to(ns[None], spread.shape)


def in_vmem(kernel, out_shapes, *args, name, smem=0):
    specs = [pl.BlockSpec(memory_space=pltpu.SMEM)] * smem
    specs += [pl.BlockSpec(memory_space=pltpu.VMEM)] * (len(args) - smem)
    return pl.pallas_call(
        kernel,
        out_shape=[jax.ShapeDtypeStruct(s, F32) for s in out_shapes],
        in_specs=specs,
        out_specs=[pl.BlockSpec(memory_space=pltpu.VMEM)] * len(out_shapes),
        name=name,
    )(*args)


def exchange(x, axes):
    return lax.all_to_all(x, axes, 0, 0, tiled=True)


def spot(yh, z, core, n_z):
    return (yh * n_z + z) * 2 + core


def moves(n_yh, n_z, kinds):
    pairs = []
    for source, target, up in kinds:
        for yh in range(n_yh - up):
            for core in range(2):
                pairs.append((spot(yh, source, core, n_z), spot(yh + up, target, core, n_z)))
    return pairs


def per_core(x):
    rows, _, _, n = x.shape
    return x.transpose(2, 0, 1, 3).reshape(2, rows, 2 * n)


def per_device(
    base_queries, adapter_input, adapter_up_weight, projected_keys, projected_values, output_gradient,
    segments, solution, residual, direction, damping,
):
    core, z, yh = lax.axis_index("core"), lax.axis_index("z"), lax.axis_index("yh")
    n_yh, n_z, n_task = lax.axis_size("yh"), lax.axis_size("z"), lax.axis_size("task")
    idx = lax.axis_index(CTX)

    def core_part(x):
        rows, feats = x.shape[0], x.shape[1] // 4
        x = x.reshape(rows, 2, 2, feats)
        return lax.dynamic_index_in_dim(x, core, 2, keepdims=False).reshape(rows, 2 * feats)

    seg = (segments[0] + 1).astype(BF16)
    width = 4 * KHALF
    kv = jnp.concatenate([projected_keys[0], projected_values[0]], axis=1)
    kv = jnp.concatenate([kv, jnp.broadcast_to(jnp.pad(seg, (0, width - BLOCK)), (SEG_ROWS, width))], axis=0)
    kv = lax.all_gather(kv, "core")
    own_rows = jnp.concatenate([core_part(kv[:, :BLOCK].reshape(CHUNK, width)[:, : width // 2]),
                                core_part(kv[:, :BLOCK].reshape(CHUNK, width)[:, width // 2 :])], axis=1)
    segs = jnp.concatenate([kv[0, BLOCK:, :BLOCK], kv[1, BLOCK:, :BLOCK], jnp.zeros((SEG_ROWS, 2 * KHALF - CHUNK), BF16)], axis=1)
    own = jnp.concatenate([own_rows, segs], axis=0)

    last = n_z - 1
    row = [(i, i + 1, 0) for i in range(last)]
    first = lax.ppermute(own, CTX, moves(n_yh, n_z, row + [(last, 0, 1)]))
    cross = lax.ppermute(own, CTX, moves(n_yh, n_z, [(last - 1, 0, 1), (last - 2, last, 1)]))
    second = lax.ppermute(first, CTX, moves(n_yh, n_z, row))
    passed = jnp.where((z == 0) | (z == last), cross, second)
    third = lax.ppermute(passed, CTX, moves(n_yh, n_z, row + [(last, 0, 0)]))
    second = jnp.where(z == 0, cross, second)

    pad = jnp.pad(adapter_input[0], ((0, 0), (0, 128 - RANK)))
    qg = jnp.concatenate(
        [
            per_core(base_queries[0].reshape(BLOCK, 2, 2, GFEAT)),
            per_core(output_gradient[0].reshape(BLOCK, 2, 2, GFEAT)),
            jnp.broadcast_to(pad[None], (2, BLOCK, 128)),
        ],
        axis=2,
    )
    qg = exchange(qg, "core").reshape(CHUNK, 2 * HALF + 128)

    up, dmat, rmat = (core_part(x.reshape(RANK, 2 * HALF)) for x in (adapter_up_weight[0], direction[0], residual[0]))
    size = direction.shape[1] // (n_yh * n_z * 2)
    parts = jnp.concatenate([lax.dynamic_slice_in_dim(x, idx * size, size, 1) for x in (solution, residual, direction)])
    consts = jnp.stack([jnp.sum(residual * residual), jnp.sum(direction * direction), jnp.sum(residual * direction), damping[0]])
    consts = jnp.pad(consts, (0, 124))[None]

    terms = attend(qg, [third, second, first, own], up, dmat, rmat)

    tail = terms[0, :1, GFEAT:]
    body = terms[:, :, :GFEAT].reshape(2, n_yh, n_z // 2, GFEAT).transpose(2, 0, 1, 3).reshape(n_z, n_yh * GFEAT)
    body = jnp.concatenate([body, jnp.broadcast_to(tail, (n_z, 128))], axis=1)
    width = body.shape[1]
    (row_sum,) = in_vmem(sum_spread_kernel, [(n_yh, 1, width)], exchange(body.reshape(n_z, 1, width), "z"), name="row_sum")
    h_all, scalars = in_vmem(
        norm_kernel, [(1, width - 128), (2 * n_z, 1, 128)], exchange(row_sum, "yh"), name="norm"
    )
    new_solution, new_residual, new_direction, spread = in_vmem(
        update_kernel,
        [(1, size)] * 3 + [(n_task, 1, size)],
        yh.reshape(1),
        exchange(scalars, ("z", "core")),
        h_all,
        consts,
        parts,
        name="update",
        smem=1,
    )
    meta_gradient = jnp.sum(exchange(spread, "task"), axis=(0, 1)) / n_task
    return new_solution, new_residual, new_direction, meta_gradient


def solution(mesh):
    n_task, n_ctx = mesh.devices.shape
    split = Mesh(mesh.devices.reshape(n_task, n_ctx // 16, 8, 2), ("task",) + CTX)
    tokens = P("task", CTX, None)
    whole = P("task", None)
    in_specs = (tokens, tokens, P("task", None, None), tokens, tokens, tokens, P("task", CTX), whole, whole, whole, P("task"))
    out_specs = (P("task", CTX), P("task", CTX), P("task", CTX), P(CTX))
    return jax.shard_map(per_device, mesh=split, in_specs=in_specs, out_specs=out_specs, check_vma=False)
```

```python
import math

import jax
import jax.numpy as jnp
from jax import lax
from jax.experimental import pallas as pl
from jax.experimental.pallas import tpu as pltpu
from jax.sharding import Mesh
from jax.sharding import PartitionSpec as P

HEAD_DIM = 128
RANK = 16
BLOCK = 128
CHUNK = 2 * BLOCK
SPAN = 3
WINDOW = 7 * BLOCK
GROUPS = 2
PER_GROUP = 4
HALF = GROUPS * PER_GROUP * HEAD_DIM
KHALF = GROUPS * HEAD_DIM
GFEAT = PER_GROUP * HEAD_DIM
ROW = GFEAT + 128
SEG_ROWS = 16
F32 = jnp.float32
BF16 = jnp.bfloat16
CTX = ("yh", "z", "core")
NT = (((1,), (1,)), ((), ()))
NN = (((1,), (0,)), ((), ()))


def dot(a, b, dims=NN):
    return lax.dot_general(a, b, dims, preferred_element_type=F32)


def fold(x):
    return x.reshape(x.shape[0] // 8, 8, x.shape[1])


def pack_kernel(keys, values, seg, out):
    n = keys.shape[1]
    out[:BLOCK, :n] = keys[...]
    out[:BLOCK, n:] = values[...]
    first = lax.broadcasted_iota(jnp.int32, (SEG_ROWS, BLOCK), 0) == 0
    row = jnp.where(first, jnp.broadcast_to(seg[...] + 1, (SEG_ROWS, BLOCK)), 0).astype(F32)
    out[BLOCK:, :BLOCK] = row.astype(BF16)
    out[BLOCK:, BLOCK:] = jnp.zeros((SEG_ROWS, out.shape[1] - BLOCK), BF16)


def attend_kernel(
    core_ref, qg, c0, c1, c2, c3, up, dmat, rmat, out, keys, keys_t, vals, qs, ts, at, qaug, s_ref, t_ref, u_ref, c_ref
):
    chunks = (c0, c1, c2, c3)
    core = core_ref[0]
    a_pad = qg[:, 2 * HALF : 2 * HALF + 128]
    a = a_pad[:, :RANK]
    qs[...] = (qg[:, :HALF].astype(F32) + dot(a, up[...])).astype(BF16)
    d = dmat[...]
    d1 = d.astype(BF16)
    rest = d - d1.astype(F32)
    d2 = rest.astype(BF16)
    d3 = (rest - d2.astype(F32)).astype(BF16)
    ts[...] = (dot(a, d1) + dot(a, d2) + dot(a, d3)).astype(BF16)
    at[...] = jnp.transpose(a_pad.astype(F32))[:RANK].astype(BF16)
    lane = lax.broadcasted_iota(jnp.int32, (BLOCK, BLOCK), 1).astype(F32)
    for j, c in enumerate(chunks):
        for half in range(2):
            rows = slice((j * 2 + half) * BLOCK, (j * 2 + half + 1) * BLOCK)
            seg_row = c[half, BLOCK:, :BLOCK].astype(F32)[0:1]
            seg = jnp.transpose(jnp.broadcast_to(seg_row, (BLOCK, BLOCK)))
            hit = seg == lane
            for g in range(GROUPS):
                col = pl.multiple_of((g * 2 + core) * HEAD_DIM, HEAD_DIM)
                k = c[half, :BLOCK, pl.ds(col, HEAD_DIM)]
                keys[g, rows, :HEAD_DIM] = k
                keys[g, rows, HEAD_DIM:] = jnp.where(hit, 1.0, 0.0).astype(BF16)
                keys_t[g, :, rows] = jnp.transpose(k.astype(F32)).astype(BF16)
                vals[g, rows, :] = c[half, :BLOCK, pl.ds(2 * KHALF + col, HEAD_DIM)]
            if j == 3:
                qaug[half] = jnp.where(hit, 0.0, -1e30).astype(BF16)
    tri = jnp.where(lax.broadcasted_iota(jnp.int32, (BLOCK, BLOCK), 0) <= lax.broadcasted_iota(jnp.int32, (BLOCK, BLOCK), 1), 0.0, -1e30)
    cexp = HEAD_DIM**-0.5 * math.log2(math.e)
    steps = [(g, b, pair) for g in range(GROUPS) for b in range(2) for pair in range(2)]

    def scores(n):
        g, b, pair = steps[n]
        slot = n % 3
        win = slice(b * BLOCK, b * BLOCK + WINDOW)
        own = slice(b * BLOCK, (b + 1) * BLOCK)

        def two(ref, base):
            cols = [base + g * GFEAT + (pair * 2 + e) * HEAD_DIM for e in range(2)]
            return [ref[own, col : col + HEAD_DIM] for col in cols]

        q2 = [jnp.concatenate([q, qaug[b]], axis=1) for q in two(qs, 0)]
        s_ref[slot] = dot(keys[g, win, :], jnp.concatenate(q2, axis=0), NT)
        t_ref[slot] = dot(keys[g, win, :HEAD_DIM], jnp.concatenate(two(ts, 0), axis=0), NT)
        u_ref[slot] = dot(vals[g, win, :], jnp.concatenate(two(qg, HALF), axis=0), NT)

    def weigh(n):
        slot = n % 3
        scales = []
        for e in range(2):
            lanes = slice(e * BLOCK, (e + 1) * BLOCK)
            m8 = None
            for w in range(6, -1, -1):
                rows = slice(w * BLOCK, (w + 1) * BLOCK)
                s = s_ref[slot, rows, lanes]
                if w == 6:
                    s = s + tri
                top = jnp.max(fold(s), axis=0)
                m8 = top if m8 is None else jnp.maximum(m8, top)
            m = jnp.max(m8, axis=0, keepdims=True)
            z8 = et8 = eu8 = etu8 = jnp.zeros((8, BLOCK), F32)
            for w in range(7):
                rows = slice(w * BLOCK, (w + 1) * BLOCK)
                s = s_ref[slot, rows, lanes]
                if w == 6:
                    s = s + tri
                ex = jnp.exp2((s - m) * cexp)
                s_ref[slot, rows, lanes] = ex
                et = ex * t_ref[slot, rows, lanes]
                u = u_ref[slot, rows, lanes]
                z8 = z8 + jnp.sum(fold(ex), axis=0)
                et8 = et8 + jnp.sum(fold(et), axis=0)
                eu8 = eu8 + jnp.sum(fold(ex * u), axis=0)
                etu8 = etu8 + jnp.sum(fold(et * u), axis=0)
            inv = 1.0 / jnp.sum(z8, axis=0, keepdims=True)
            mt = jnp.sum(et8, axis=0, keepdims=True) * inv
            mu = jnp.sum(eu8, axis=0, keepdims=True) * inv
            cov = jnp.sum(etu8, axis=0, keepdims=True) * inv - mt * mu
            for w in range(7):
                rows = slice(w * BLOCK, (w + 1) * BLOCK)
                coef = s_ref[slot, rows, lanes] * (
                    (t_ref[slot, rows, lanes] - mt) * (u_ref[slot, rows, lanes] - mu) - cov
                )
                c_ref[slot, rows, lanes] = coef.astype(BF16)
            scales.append(inv * (1.0 / HEAD_DIM))
        return scales

    def gather(n, scales):
        g, b, pair = steps[n]
        slot = n % 3
        hv = dot(keys_t[g, :, b * BLOCK : b * BLOCK + WINDOW], c_ref[slot])
        ab = at[:, b * BLOCK : (b + 1) * BLOCK]
        for e in range(2):
            lanes = slice(e * BLOCK, (e + 1) * BLOCK)
            head = (hv[:, lanes] * scales[e]).astype(BF16)
            left = g * ROW + (pair * 2 + e) * HEAD_DIM
            cols = slice(left, left + HEAD_DIM)
            part = dot(ab, head, NT)
            if b == 0:
                out[:, cols] = part
            else:
                out[:, cols] += part

    scores(0)
    for n in range(8):
        if n < 7:
            scores(n + 1)
        gather(n, weigh(n))
    dh = rh = jnp.zeros((1, 1), F32)
    for g in range(GROUPS):
        h = out[:, g * ROW : g * ROW + GFEAT]
        cols = slice(g * GFEAT, (g + 1) * GFEAT)
        dh = dh + jnp.sum(h * d[:, cols], keepdims=True)
        rh = rh + jnp.sum(h * rmat[:, cols], keepdims=True)
    lane = lax.broadcasted_iota(jnp.int32, (RANK, 128), 1)
    tail = jnp.where(lane == 0, dh, jnp.where(lane == 1, rh, 0.0))
    for g in range(GROUPS):
        out[:, g * ROW + GFEAT : (g + 1) * ROW] = tail


def attend(core, qg, chunks, up, dmat, rmat):
    vm = pltpu.VMEM
    return pl.pallas_call(
        attend_kernel,
        out_shape=jax.ShapeDtypeStruct((RANK, GROUPS * ROW), F32),
        in_specs=[pl.BlockSpec(memory_space=pltpu.SMEM)] + [pl.BlockSpec(memory_space=vm)] * 8,
        out_specs=pl.BlockSpec(memory_space=vm),
        scratch_shapes=[
            vm((GROUPS, 4 * CHUNK, 2 * HEAD_DIM), BF16),
            vm((GROUPS, HEAD_DIM, 4 * CHUNK), BF16),
            vm((GROUPS, 4 * CHUNK, HEAD_DIM), BF16),
            vm((CHUNK, HALF), BF16),
            vm((CHUNK, HALF), BF16),
            vm((RANK, CHUNK), BF16),
            vm((2, BLOCK, BLOCK), BF16),
            vm((3, WINDOW, CHUNK), F32),
            vm((3, WINDOW, CHUNK), F32),
            vm((3, WINDOW, CHUNK), F32),
            vm((3, WINDOW, CHUNK), BF16),
        ],
        compiler_params=pltpu.CompilerParams(vmem_limit_bytes=48 * 1024 * 1024),
        cost_estimate=pl.CostEstimate(flops=2_000_000_000, bytes_accessed=4_000_000, transcendentals=2_000_000),
        name="attend",
    )(core, qg, *chunks, up, dmat, rmat)


def norm_kernel(got, h_out, out):
    total = jnp.sum(got[...], axis=0)
    h = total[:, : h_out.shape[1]]
    h_out[...] = h
    tail = total[:, h_out.shape[1] :]
    lane = lax.broadcasted_iota(jnp.int32, tail.shape, 1)
    share = 2.0 / out.shape[0]
    row = jnp.where(lane == 2, jnp.sum(h * h, keepdims=True), tail * share)
    out[...] = jnp.broadcast_to(row[None], out.shape)


def update_kernel(got, h_all, dot_in, parts, new_solution, new_residual, new_direction, spread):
    total = jnp.sum(got[...], axis=0)
    lane = lax.broadcasted_iota(jnp.int32, total.shape, 1)

    def pick(row, k):
        return jnp.sum(jnp.where(lane == k, row, 0.0), keepdims=True)

    dh, rh, hh = pick(total, 0), pick(total, 1), pick(total, 2)
    consts = dot_in[...]
    rr, dd, rd, damp = (pick(consts, k) for k in range(4))
    h = h_all[...]
    sol, res, dirn = parts[0:1], parts[1:2], parts[2:3]
    step_len = rr / (dd + dh / damp)
    curved = dirn + h / damp
    rc = rd + rh / damp
    cc = dd + 2.0 * dh / damp + hh / (damp * damp)
    new_norm = rr - 2.0 * step_len * rc + step_len * step_len * cc
    ns = sol + step_len * dirn
    nr = res - step_len * curved
    new_solution[...] = ns
    new_residual[...] = nr
    new_direction[...] = nr + (new_norm / rr) * dirn
    spread[...] = jnp.broadcast_to(ns[None], spread.shape)


def in_vmem(kernel, out_shapes, *args, name, dtype=F32):
    return pl.pallas_call(
        kernel,
        out_shape=[jax.ShapeDtypeStruct(s, dtype) for s in out_shapes],
        in_specs=[pl.BlockSpec(memory_space=pltpu.VMEM)] * len(args),
        out_specs=[pl.BlockSpec(memory_space=pltpu.VMEM)] * len(out_shapes),
        name=name,
    )(*args)


def exchange(x, axes):
    return lax.all_to_all(x, axes, 0, 0, tiled=True)


def spot(yh, z, core, n_z):
    return (yh * n_z + z) * 2 + core


def moves(n_yh, n_z, kinds):
    pairs = []
    for source, target, up in kinds:
        for yh in range(n_yh - up):
            for core in range(2):
                pairs.append((spot(yh, source, core, n_z), spot(yh + up, target, core, n_z)))
    return pairs


def per_core(x):
    rows, _, _, n = x.shape
    return x.transpose(2, 0, 1, 3).reshape(2, rows, 2 * n)


def per_device(
    base_queries, adapter_input, adapter_up_weight, projected_keys, projected_values, output_gradient,
    segments, solution, residual, direction, damping,
):
    core, z = lax.axis_index("core"), lax.axis_index("z")
    n_yh, n_z, n_task = lax.axis_size("yh"), lax.axis_size("z"), lax.axis_size("task")
    idx = lax.axis_index(CTX)

    def core_part(x):
        rows, feats = x.shape[0], x.shape[1] // 4
        x = x.reshape(rows, 2, 2, feats)
        return lax.dynamic_index_in_dim(x, core, 2, keepdims=False).reshape(rows, 2 * feats)

    last = n_z - 1
    row = [(i, i + 1, 0) for i in range(last)]

    def move(x, *kinds):
        return lax.ppermute(x, CTX, moves(n_yh, n_z, kinds))

    (own,) = in_vmem(
        pack_kernel, [(BLOCK + SEG_ROWS, 4 * KHALF)], projected_keys[0], projected_values[0], segments, name="pack", dtype=BF16
    )
    first = move(own, *row, (last, 0, 1))
    cross = move(own, (last - 1, last, 1), (last - 2, last - 1, 1))
    second = move(jnp.where(z == last, cross, first), *row, (last, 0, 0))
    cross = move(cross, (last - 1, last, 0))
    third = move(jnp.where(z == last, cross, second), *row, (last, 0, 0))
    chunks = [lax.all_gather(x, "core") for x in (third, second, first, own)]

    pad = jnp.pad(adapter_input[0], ((0, 0), (0, 128 - RANK)))
    qg = jnp.concatenate(
        [
            per_core(base_queries[0].reshape(BLOCK, 2, 2, GFEAT)),
            per_core(output_gradient[0].reshape(BLOCK, 2, 2, GFEAT)),
            jnp.broadcast_to(pad[None], (2, BLOCK, 128)),
        ],
        axis=2,
    )
    qg = exchange(qg, "core").reshape(CHUNK, 2 * HALF + 128)

    up, dmat, rmat = (core_part(x.reshape(RANK, 2 * HALF)) for x in (adapter_up_weight[0], direction[0], residual[0]))
    size = direction.shape[1] // (n_yh * n_z * 2)
    parts = jnp.concatenate([lax.dynamic_slice_in_dim(x, idx * size, size, 1) for x in (solution, residual, direction)])
    consts = jnp.stack([jnp.sum(residual * residual), jnp.sum(direction * direction), jnp.sum(residual * direction), damping[0]])
    consts = jnp.pad(consts, (0, 124))[None]

    terms = attend(core.reshape(1), qg, chunks, up, dmat, rmat)

    peers = n_yh * n_z
    h, scalars = in_vmem(
        norm_kernel, [(1, GFEAT), (2 * peers, 1, 128)], exchange(terms.reshape(peers, 1, ROW), ("yh", "z")), name="norm"
    )
    new_solution, new_residual, new_direction, spread = in_vmem(
        update_kernel, [(1, size)] * 3 + [(n_task, 1, size)], exchange(scalars, CTX), h, consts, parts, name="update"
    )
    meta_gradient = jnp.sum(exchange(spread, "task"), axis=(0, 1)) / n_task
    return new_solution, new_residual, new_direction, meta_gradient


def solution(mesh):
    n_task, n_ctx = mesh.devices.shape
    split = Mesh(mesh.devices.reshape(n_task, n_ctx // 16, 8, 2), ("task",) + CTX)
    tokens = P("task", CTX, None)
    whole = P("task", None)
    in_specs = (tokens, tokens, P("task", None, None), tokens, tokens, tokens, P("task", CTX), whole, whole, whole, P("task"))
    out_specs = (P("task", CTX), P("task", CTX), P("task", CTX), P(CTX))
    return jax.shard_map(per_device, mesh=split, in_specs=in_specs, out_specs=out_specs, check_vma=False)
```

```python
import math

import jax
import jax.numpy as jnp
from jax import lax
from jax.experimental import pallas as pl
from jax.experimental.pallas import tpu as pltpu
from jax.sharding import Mesh
from jax.sharding import PartitionSpec as P

HEAD_DIM = 128
RANK = 16
BLOCK = 128
CHUNK = 2 * BLOCK
SPAN = 3
WINDOW = 7 * BLOCK
GROUPS = 2
PER_GROUP = 4
HALF = GROUPS * PER_GROUP * HEAD_DIM
KHALF = GROUPS * HEAD_DIM
GFEAT = PER_GROUP * HEAD_DIM
ROW = GFEAT + 128
SEG_ROWS = 16
F32 = jnp.float32
BF16 = jnp.bfloat16
CTX = ("yh", "z", "core")
NT = (((1,), (1,)), ((), ()))
NN = (((1,), (0,)), ((), ()))


def dot(a, b, dims=NN):
    return lax.dot_general(a, b, dims, preferred_element_type=F32)


def fold(x):
    return x.reshape(x.shape[0] // 8, 8, x.shape[1])


def pack_kernel(keys, values, seg, out):
    n = keys.shape[1]
    out[:BLOCK, :n] = keys[...]
    out[:BLOCK, n:] = values[...]
    first = lax.broadcasted_iota(jnp.int32, (SEG_ROWS, BLOCK), 0) == 0
    row = jnp.where(first, jnp.broadcast_to(seg[...] + 1, (SEG_ROWS, BLOCK)), 0).astype(F32)
    out[BLOCK:, :BLOCK] = row.astype(BF16)
    out[BLOCK:, BLOCK:] = jnp.zeros((SEG_ROWS, out.shape[1] - BLOCK), BF16)


def pack_queries_kernel(queries, grads, adapter_t, out):
    a = jnp.concatenate([adapter_t[...].astype(F32), jnp.zeros((BLOCK - RANK, BLOCK), F32)], axis=0)
    a = jnp.transpose(a).astype(BF16)
    for core in range(2):
        for i, ref in enumerate((queries, grads)):
            for g in range(GROUPS):
                to, at = i * HALF + g * GFEAT, (g * 2 + core) * GFEAT
                out[core, :, to : to + GFEAT] = ref[:, at : at + GFEAT]
        out[core, :, 2 * HALF :] = a


def attend_kernel(
    core_ref, qg, far, c1, c2, c3, up, dmat, rmat, out, c0, sem, keys, keys_t, vals, qs, ts, at, qaug, s_ref, t_ref, u_ref, c_ref
):
    chunks = (c0, c1, c2, c3)
    core = core_ref[0]
    copy = pltpu.make_async_copy(far, c0, sem)
    copy.start()

    def mine(ref):
        parts = [ref[:, pl.ds(pl.multiple_of((g * 2 + core) * GFEAT, GFEAT), GFEAT)] for g in range(GROUPS)]
        return jnp.concatenate(parts, axis=1)

    a_pad = qg[:, 2 * HALF : 2 * HALF + 128]
    a = a_pad[:, :RANK]
    qs[...] = (qg[:, :HALF].astype(F32) + dot(a, mine(up))).astype(BF16)
    d, r = mine(dmat), mine(rmat)
    d1 = d.astype(BF16)
    rest = d - d1.astype(F32)
    d2 = rest.astype(BF16)
    d3 = (rest - d2.astype(F32)).astype(BF16)
    ts[...] = (dot(a, d1) + dot(a, d2) + dot(a, d3)).astype(BF16)
    at[...] = jnp.transpose(a_pad.astype(F32))[:RANK].astype(BF16)
    lane = lax.broadcasted_iota(jnp.int32, (BLOCK, BLOCK), 1).astype(F32)
    for j in (3, 2, 1, 0):
        c = chunks[j]
        if j == 0:
            copy.wait()
        for half in range(2):
            rows = slice((j * 2 + half) * BLOCK, (j * 2 + half + 1) * BLOCK)
            seg_row = c[half, BLOCK:, :BLOCK].astype(F32)[0:1]
            seg = jnp.transpose(jnp.broadcast_to(seg_row, (BLOCK, BLOCK)))
            hit = seg == lane
            for g in range(GROUPS):
                col = pl.multiple_of((g * 2 + core) * HEAD_DIM, HEAD_DIM)
                k = c[half, :BLOCK, pl.ds(col, HEAD_DIM)]
                keys[g, rows, :HEAD_DIM] = k
                keys[g, rows, HEAD_DIM:] = jnp.where(hit, 1.0, 0.0).astype(BF16)
                keys_t[g, :, rows] = jnp.transpose(k.astype(F32)).astype(BF16)
                vals[g, rows, :] = c[half, :BLOCK, pl.ds(2 * KHALF + col, HEAD_DIM)]
            if j == 3:
                qaug[half] = jnp.where(hit, 0.0, -1e30).astype(BF16)
    tri = jnp.where(lax.broadcasted_iota(jnp.int32, (BLOCK, BLOCK), 0) <= lax.broadcasted_iota(jnp.int32, (BLOCK, BLOCK), 1), 0.0, -1e30)
    cexp = HEAD_DIM**-0.5 * math.log2(math.e)
    steps = [(g, b, pair) for g in range(GROUPS) for b in range(2) for pair in range(2)]

    def scores(n):
        g, b, pair = steps[n]
        slot = n % 3
        win = slice(b * BLOCK, b * BLOCK + WINDOW)
        own = slice(b * BLOCK, (b + 1) * BLOCK)

        def two(ref, base):
            cols = [base + g * GFEAT + (pair * 2 + e) * HEAD_DIM for e in range(2)]
            return [ref[own, col : col + HEAD_DIM] for col in cols]

        q2 = [jnp.concatenate([q, qaug[b]], axis=1) for q in two(qs, 0)]
        q, t, r = (jnp.concatenate(x, axis=0) for x in (q2, two(ts, 0), two(qg, HALF)))

        def do_s():
            s_ref[slot] = dot(keys[g, win, :], q, NT)

        def do_t():
            t_ref[slot] = dot(keys[g, win, :HEAD_DIM], t, NT)

        def do_u():
            u_ref[slot] = dot(vals[g, win, :], r, NT)

        return [do_s, do_t, do_u]

    def weigh(n, ahead):
        slot = n % 3
        scales = []
        for e in range(2):
            lanes = slice(e * BLOCK, (e + 1) * BLOCK)
            m8 = None
            for w in range(6, -1, -1):
                rows = slice(w * BLOCK, (w + 1) * BLOCK)
                s = s_ref[slot, rows, lanes]
                if w == 6:
                    s = s + tri
                top = jnp.max(fold(s), axis=0)
                m8 = top if m8 is None else jnp.maximum(m8, top)
            m = jnp.max(m8, axis=0, keepdims=True)
            if ahead:
                ahead.pop(0)()
            z8 = et8 = eu8 = etu8 = jnp.zeros((8, BLOCK), F32)
            for w in range(7):
                rows = slice(w * BLOCK, (w + 1) * BLOCK)
                s = s_ref[slot, rows, lanes]
                if w == 6:
                    s = s + tri
                ex = jnp.exp2((s - m) * cexp)
                s_ref[slot, rows, lanes] = ex
                et = ex * t_ref[slot, rows, lanes]
                u = u_ref[slot, rows, lanes]
                z8 = z8 + jnp.sum(fold(ex), axis=0)
                et8 = et8 + jnp.sum(fold(et), axis=0)
                eu8 = eu8 + jnp.sum(fold(ex * u), axis=0)
                etu8 = etu8 + jnp.sum(fold(et * u), axis=0)
            inv = 1.0 / jnp.sum(z8, axis=0, keepdims=True)
            mt = jnp.sum(et8, axis=0, keepdims=True) * inv
            mu = jnp.sum(eu8, axis=0, keepdims=True) * inv
            cov = jnp.sum(etu8, axis=0, keepdims=True) * inv - mt * mu
            for w in range(7):
                rows = slice(w * BLOCK, (w + 1) * BLOCK)
                coef = s_ref[slot, rows, lanes] * (
                    (t_ref[slot, rows, lanes] - mt) * (u_ref[slot, rows, lanes] - mu) - cov
                )
                c_ref[slot, rows, lanes] = coef.astype(BF16)
            if ahead:
                ahead.pop(0)()
            scales.append(inv * (1.0 / HEAD_DIM))
        return scales

    def gather(n, scales):
        g, b, pair = steps[n]
        slot = n % 3
        hv = dot(keys_t[g, :, b * BLOCK : b * BLOCK + WINDOW], c_ref[slot])
        ab = at[:, b * BLOCK : (b + 1) * BLOCK]
        for e in range(2):
            lanes = slice(e * BLOCK, (e + 1) * BLOCK)
            head = (hv[:, lanes] * scales[e]).astype(BF16)
            left = g * ROW + (pair * 2 + e) * HEAD_DIM
            cols = slice(left, left + HEAD_DIM)
            part = dot(ab, head, NT)
            if b == 0:
                out[:, cols] = part
            else:
                out[:, cols] += part

    for matmul in scores(0):
        matmul()
    for n in range(8):
        gather(n, weigh(n, scores(n + 1) if n < 7 else []))
    h = jnp.concatenate([out[:, g * ROW : g * ROW + GFEAT] for g in range(GROUPS)], axis=1)
    lane = lax.broadcasted_iota(jnp.int32, (RANK, 128), 1)
    tail = jnp.zeros((RANK, 128), F32)
    share = 1.0 / (RANK * GROUPS)
    for k, term in enumerate((h * d, h * r, r * r * share, d * d * share, r * d * share)):
        tail = jnp.where(lane == k, jnp.sum(term, keepdims=True), tail)
    for g in range(GROUPS):
        out[:, g * ROW + GFEAT : (g + 1) * ROW] = tail


def attend(core, qg, chunks, up, dmat, rmat):
    vm = pltpu.VMEM
    return pl.pallas_call(
        attend_kernel,
        out_shape=jax.ShapeDtypeStruct((RANK, GROUPS * ROW), F32),
        in_specs=[pl.BlockSpec(memory_space=x) for x in (pltpu.SMEM, vm, pl.ANY, vm, vm, vm, vm, vm, vm)],
        out_specs=pl.BlockSpec(memory_space=vm),
        scratch_shapes=[
            vm((2, BLOCK + SEG_ROWS, 4 * KHALF), BF16),
            pltpu.SemaphoreType.DMA,
            vm((GROUPS, 4 * CHUNK, 2 * HEAD_DIM), BF16),
            vm((GROUPS, HEAD_DIM, 4 * CHUNK), BF16),
            vm((GROUPS, 4 * CHUNK, HEAD_DIM), BF16),
            vm((CHUNK, HALF), BF16),
            vm((CHUNK, HALF), BF16),
            vm((RANK, CHUNK), BF16),
            vm((2, BLOCK, BLOCK), BF16),
            vm((3, WINDOW, CHUNK), F32),
            vm((3, WINDOW, CHUNK), F32),
            vm((3, WINDOW, CHUNK), F32),
            vm((3, WINDOW, CHUNK), BF16),
        ],
        compiler_params=pltpu.CompilerParams(vmem_limit_bytes=48 * 1024 * 1024),
        cost_estimate=pl.CostEstimate(flops=2_000_000_000, bytes_accessed=4_000_000, transcendentals=2_000_000),
        name="attend",
    )(core, qg, *chunks, up, dmat, rmat)


def norm_kernel(got, h_out, out):
    total = jnp.sum(got[...], axis=0)
    h = total[:, : h_out.shape[1]]
    h_out[...] = h
    tail = total[:, h_out.shape[1] :]
    lane = lax.broadcasted_iota(jnp.int32, tail.shape, 1)
    share = 2.0 / out.shape[0]
    row = jnp.where(lane == 5, jnp.sum(h * h, keepdims=True), tail * share)
    out[...] = jnp.broadcast_to(row[None], out.shape)


def update_kernel(damping, got, h_all, parts, new_solution, new_residual, new_direction, spread):
    total = jnp.sum(got[...], axis=0)
    lane = lax.broadcasted_iota(jnp.int32, total.shape, 1)

    def pick(row, k):
        return jnp.sum(jnp.where(lane == k, row, 0.0), keepdims=True)

    dh, rh, rr, dd, rd, hh = (pick(total, k) for k in range(6))
    damp = damping[0]
    h = h_all[...]
    sol, res, dirn = parts[0:1], parts[1:2], parts[2:3]
    step_len = rr / (dd + dh / damp)
    curved = dirn + h / damp
    rc = rd + rh / damp
    cc = dd + 2.0 * dh / damp + hh / (damp * damp)
    new_norm = rr - 2.0 * step_len * rc + step_len * step_len * cc
    ns = sol + step_len * dirn
    nr = res - step_len * curved
    new_solution[...] = ns
    new_residual[...] = nr
    new_direction[...] = nr + (new_norm / rr) * dirn
    spread[...] = jnp.broadcast_to(ns[None], spread.shape)


def in_vmem(kernel, out_shapes, *args, name, dtype=F32, smem=0):
    return pl.pallas_call(
        kernel,
        out_shape=[jax.ShapeDtypeStruct(s, dtype) for s in out_shapes],
        in_specs=[pl.BlockSpec(memory_space=pltpu.SMEM if i < smem else pltpu.VMEM) for i in range(len(args))],
        out_specs=[pl.BlockSpec(memory_space=pltpu.VMEM)] * len(out_shapes),
        name=name,
    )(*args)


def exchange(x, axes):
    return lax.all_to_all(x, axes, 0, 0, tiled=True)


def spot(yh, z, core, n_z):
    return (yh * n_z + z) * 2 + core


def moves(n_yh, n_z, kinds):
    pairs = []
    for source, target, up in kinds:
        for yh in range(n_yh - up):
            for core in range(2):
                pairs.append((spot(yh, source, core, n_z), spot(yh + up, target, core, n_z)))
    return pairs


def per_device(
    base_queries, adapter_input, adapter_up_weight, projected_keys, projected_values, output_gradient,
    segments, solution, residual, direction, damping,
):
    core, z = lax.axis_index("core"), lax.axis_index("z")
    n_yh, n_z, n_task = lax.axis_size("yh"), lax.axis_size("z"), lax.axis_size("task")
    idx = lax.axis_index(CTX)

    last = n_z - 1
    row = [(i, i + 1, 0) for i in range(last)]

    def move(x, *kinds):
        return lax.ppermute(x, CTX, moves(n_yh, n_z, kinds))

    (own,) = in_vmem(
        pack_kernel, [(BLOCK + SEG_ROWS, 4 * KHALF)], projected_keys[0], projected_values[0], segments, name="pack", dtype=BF16
    )
    (qg,) = in_vmem(
        pack_queries_kernel, [(2, BLOCK, 2 * HALF + 128)], base_queries[0], output_gradient[0], adapter_input[0].T,
        name="pack_queries", dtype=BF16,
    )
    first = move(own, *row, (last, 0, 1))
    cross = move(own, (last - 1, 0, 1), (last - 2, last, 1))
    first, own, qg = lax.optimization_barrier((first, own, qg))
    second = move(first, *row)
    qg = exchange(qg, "core").reshape(CHUNK, 2 * HALF + 128)
    passed = jnp.where((z == 0) | (z == last), cross, second)
    third = move(passed, *row, (last, 0, 0))
    second = jnp.where(z == 0, cross, second)
    chunks = [lax.all_gather(x, "core") for x in (third, second, first, own)]

    size = direction.shape[1] // (n_yh * n_z * 2)
    parts = jnp.concatenate([lax.dynamic_slice_in_dim(x, idx * size, size, 1) for x in (solution, residual, direction)])

    up, dmat, rmat = (x.reshape(RANK, 2 * HALF) for x in (adapter_up_weight, direction, residual))
    terms = attend(core.reshape(1), qg, chunks, up, dmat, rmat)

    peers = n_yh * n_z
    h, scalars = in_vmem(
        norm_kernel, [(1, GFEAT), (2 * peers, 1, 128)], exchange(terms.reshape(peers, 1, ROW), ("yh", "z")), name="norm"
    )
    new_solution, new_residual, new_direction, spread = in_vmem(
        update_kernel, [(1, size)] * 3 + [(n_task, 1, size)], damping, exchange(scalars, CTX), h, parts, name="update", smem=1
    )
    meta_gradient = jnp.sum(exchange(spread, "task"), axis=(0, 1)) / n_task
    return new_solution, new_residual, new_direction, meta_gradient


def solution(mesh):
    n_task, n_ctx = mesh.devices.shape
    split = Mesh(mesh.devices.reshape(n_task, n_ctx // 16, 8, 2), ("task",) + CTX)
    tokens = P("task", CTX, None)
    whole = P("task", None)
    in_specs = (tokens, tokens, P("task", None, None), tokens, tokens, tokens, P("task", CTX), whole, whole, whole, P("task"))
    out_specs = (P("task", CTX), P("task", CTX), P("task", CTX), P(CTX))
    return jax.shard_map(per_device, mesh=split, in_specs=in_specs, out_specs=out_specs, check_vma=False)
```

```python
import math

import jax
import jax.numpy as jnp
from jax import lax
from jax.experimental import pallas as pl
from jax.experimental.pallas import tpu as pltpu
from jax.sharding import Mesh
from jax.sharding import PartitionSpec as P

HEAD_DIM = 128
RANK = 16
BLOCK = 128
CHUNK = 2 * BLOCK
SPAN = 3
WINDOW = 7 * BLOCK
GROUPS = 2
PER_GROUP = 4
HALF = GROUPS * PER_GROUP * HEAD_DIM
KHALF = GROUPS * HEAD_DIM
GFEAT = PER_GROUP * HEAD_DIM
ROW = GFEAT + 128
SEG_ROWS = 16
F32 = jnp.float32
BF16 = jnp.bfloat16
CTX = ("yh", "z", "core")
NT = (((1,), (1,)), ((), ()))
NN = (((1,), (0,)), ((), ()))


def dot(a, b, dims=NN):
    return lax.dot_general(a, b, dims, preferred_element_type=F32)


def fold(x):
    return x.reshape(x.shape[0] // 8, 8, x.shape[1])


def pack_kernel(keys, values, seg, out):
    n = keys.shape[1]
    out[:BLOCK, :n] = keys[...]
    out[:BLOCK, n:] = values[...]
    first = lax.broadcasted_iota(jnp.int32, (SEG_ROWS, BLOCK), 0) == 0
    row = jnp.where(first, jnp.broadcast_to(seg[...] + 1, (SEG_ROWS, BLOCK)), 0).astype(F32)
    out[BLOCK:, :BLOCK] = row.astype(BF16)
    out[BLOCK:, BLOCK:] = jnp.zeros((SEG_ROWS, out.shape[1] - BLOCK), BF16)


def pack_queries_kernel(queries, grads, adapter_t, out):
    a = jnp.concatenate([adapter_t[...].astype(F32), jnp.zeros((BLOCK - RANK, BLOCK), F32)], axis=0)
    a = jnp.transpose(a).astype(BF16)
    for core in range(2):
        for i, ref in enumerate((queries, grads)):
            for g in range(GROUPS):
                to, at = i * HALF + g * GFEAT, (g * 2 + core) * GFEAT
                out[core, :, to : to + GFEAT] = ref[:, at : at + GFEAT]
        out[core, :, 2 * HALF :] = a


def attend_kernel(
    core_ref, qg, far, c1, c2, c3, up, dmat, rmat, out, c0, sem, keys, keys_t, vals, qs, ts, at, qaug, s_ref, t_ref, u_ref, c_ref
):
    chunks = (c0, c1, c2, c3)
    core = core_ref[0]
    copy = pltpu.make_async_copy(far, c0, sem)
    copy.start()

    def mine(ref):
        parts = [ref[:, pl.ds(pl.multiple_of((g * 2 + core) * GFEAT, GFEAT), GFEAT)] for g in range(GROUPS)]
        return jnp.concatenate(parts, axis=1)

    a_pad = qg[:, 2 * HALF : 2 * HALF + 128]
    a = a_pad[:, :RANK]
    qs[...] = (qg[:, :HALF].astype(F32) + dot(a, mine(up))).astype(BF16)
    d, r = mine(dmat), mine(rmat)
    d1 = d.astype(BF16)
    rest = d - d1.astype(F32)
    d2 = rest.astype(BF16)
    d3 = (rest - d2.astype(F32)).astype(BF16)
    ts[...] = (dot(a, d1) + dot(a, d2) + dot(a, d3)).astype(BF16)
    at[...] = jnp.transpose(a_pad.astype(F32))[:RANK].astype(BF16)
    lane = lax.broadcasted_iota(jnp.int32, (BLOCK, BLOCK), 1).astype(F32)
    for j in (3, 2, 1, 0):
        c = chunks[j]
        if j == 0:
            copy.wait()
        for half in range(2):
            rows = slice((j * 2 + half) * BLOCK, (j * 2 + half + 1) * BLOCK)
            seg_row = c[half, BLOCK:, :BLOCK].astype(F32)[0:1]
            seg = jnp.transpose(jnp.broadcast_to(seg_row, (BLOCK, BLOCK)))
            hit = seg == lane
            for g in range(GROUPS):
                col = pl.multiple_of((g * 2 + core) * HEAD_DIM, HEAD_DIM)
                k = c[half, :BLOCK, pl.ds(col, HEAD_DIM)]
                keys[g, rows, :HEAD_DIM] = k
                keys[g, rows, HEAD_DIM:] = jnp.where(hit, 1.0, 0.0).astype(BF16)
                keys_t[g, :, rows] = jnp.transpose(k.astype(F32)).astype(BF16)
                vals[g, rows, :] = c[half, :BLOCK, pl.ds(2 * KHALF + col, HEAD_DIM)]
            if j == 3:
                qaug[half] = jnp.where(hit, 0.0, -1e30).astype(BF16)
    tri = jnp.where(lax.broadcasted_iota(jnp.int32, (BLOCK, BLOCK), 0) <= lax.broadcasted_iota(jnp.int32, (BLOCK, BLOCK), 1), 0.0, -1e30)
    cexp = HEAD_DIM**-0.5 * math.log2(math.e)
    steps = [(g, b, pair) for g in range(GROUPS) for b in range(2) for pair in range(2)]

    def scores(n):
        g, b, pair = steps[n]
        slot = n % 3
        win = slice(b * BLOCK, b * BLOCK + WINDOW)
        own = slice(b * BLOCK, (b + 1) * BLOCK)

        def two(ref, base):
            cols = [base + g * GFEAT + (pair * 2 + e) * HEAD_DIM for e in range(2)]
            return [ref[own, col : col + HEAD_DIM] for col in cols]

        q2 = [jnp.concatenate([q, qaug[b]], axis=1) for q in two(qs, 0)]
        q, t, r = (jnp.concatenate(x, axis=0) for x in (q2, two(ts, 0), two(qg, HALF)))

        def do_s():
            s_ref[slot] = dot(keys[g, win, :], q, NT)

        def do_t():
            t_ref[slot] = dot(keys[g, win, :HEAD_DIM], t, NT)

        def do_u():
            u_ref[slot] = dot(vals[g, win, :], r, NT)

        return [do_s, do_t, do_u]

    def weigh(n, ahead):
        slot = n % 3
        scales = []
        for e in range(2):
            lanes = slice(e * BLOCK, (e + 1) * BLOCK)
            m8 = None
            for w in range(6, -1, -1):
                rows = slice(w * BLOCK, (w + 1) * BLOCK)
                s = s_ref[slot, rows, lanes]
                if w == 6:
                    s = s + tri
                top = jnp.max(fold(s), axis=0)
                m8 = top if m8 is None else jnp.maximum(m8, top)
            m = jnp.max(m8, axis=0, keepdims=True)
            if ahead:
                ahead.pop(0)()
            z8 = et8 = eu8 = etu8 = jnp.zeros((8, BLOCK), F32)
            for w in range(7):
                rows = slice(w * BLOCK, (w + 1) * BLOCK)
                s = s_ref[slot, rows, lanes]
                if w == 6:
                    s = s + tri
                ex = jnp.exp2((s - m) * cexp)
                s_ref[slot, rows, lanes] = ex
                et = ex * t_ref[slot, rows, lanes]
                u = u_ref[slot, rows, lanes]
                z8 = z8 + jnp.sum(fold(ex), axis=0)
                et8 = et8 + jnp.sum(fold(et), axis=0)
                eu8 = eu8 + jnp.sum(fold(ex * u), axis=0)
                etu8 = etu8 + jnp.sum(fold(et * u), axis=0)
            inv = 1.0 / jnp.sum(z8, axis=0, keepdims=True)
            mt = jnp.sum(et8, axis=0, keepdims=True) * inv
            mu = jnp.sum(eu8, axis=0, keepdims=True) * inv
            cov = jnp.sum(etu8, axis=0, keepdims=True) * inv - mt * mu
            for w in range(7):
                rows = slice(w * BLOCK, (w + 1) * BLOCK)
                coef = s_ref[slot, rows, lanes] * (
                    (t_ref[slot, rows, lanes] - mt) * (u_ref[slot, rows, lanes] - mu) - cov
                )
                c_ref[slot, rows, lanes] = coef.astype(BF16)
            if ahead:
                ahead.pop(0)()
            scales.append(inv * (1.0 / HEAD_DIM))
        return scales

    def gather(n, scales):
        g, b, pair = steps[n]
        slot = n % 3
        hv = dot(keys_t[g, :, b * BLOCK : b * BLOCK + WINDOW], c_ref[slot])
        ab = at[:, b * BLOCK : (b + 1) * BLOCK]
        for e in range(2):
            lanes = slice(e * BLOCK, (e + 1) * BLOCK)
            head = (hv[:, lanes] * scales[e]).astype(BF16)
            left = g * ROW + (pair * 2 + e) * HEAD_DIM
            cols = slice(left, left + HEAD_DIM)
            part = dot(ab, head, NT)
            if b == 0:
                out[:, cols] = part
            else:
                out[:, cols] += part

    for matmul in scores(0):
        matmul()
    for n in range(8):
        gather(n, weigh(n, scores(n + 1) if n < 7 else []))
    h = jnp.concatenate([out[:, g * ROW : g * ROW + GFEAT] for g in range(GROUPS)], axis=1)
    lane = lax.broadcasted_iota(jnp.int32, (RANK, 128), 1)
    tail = jnp.zeros((RANK, 128), F32)
    share = 1.0 / (RANK * GROUPS)
    for k, term in enumerate((h * d, h * r, r * r * share, d * d * share, r * d * share)):
        tail = jnp.where(lane == k, jnp.sum(term, keepdims=True), tail)
    for g in range(GROUPS):
        out[:, g * ROW + GFEAT : (g + 1) * ROW] = tail


def attend(core, qg, chunks, up, dmat, rmat):
    vm = pltpu.VMEM
    return pl.pallas_call(
        attend_kernel,
        out_shape=jax.ShapeDtypeStruct((RANK, GROUPS * ROW), F32),
        in_specs=[pl.BlockSpec(memory_space=x) for x in (pltpu.SMEM, vm, pl.ANY, vm, vm, vm, vm, vm, vm)],
        out_specs=pl.BlockSpec(memory_space=vm),
        scratch_shapes=[
            vm((2, BLOCK + SEG_ROWS, 4 * KHALF), BF16),
            pltpu.SemaphoreType.DMA,
            vm((GROUPS, 4 * CHUNK, 2 * HEAD_DIM), BF16),
            vm((GROUPS, HEAD_DIM, 4 * CHUNK), BF16),
            vm((GROUPS, 4 * CHUNK, HEAD_DIM), BF16),
            vm((CHUNK, HALF), BF16),
            vm((CHUNK, HALF), BF16),
            vm((RANK, CHUNK), BF16),
            vm((2, BLOCK, BLOCK), BF16),
            vm((3, WINDOW, CHUNK), F32),
            vm((3, WINDOW, CHUNK), F32),
            vm((3, WINDOW, CHUNK), F32),
            vm((3, WINDOW, CHUNK), BF16),
        ],
        compiler_params=pltpu.CompilerParams(vmem_limit_bytes=48 * 1024 * 1024),
        cost_estimate=pl.CostEstimate(flops=2_000_000_000, bytes_accessed=4_000_000, transcendentals=2_000_000),
        name="attend",
    )(core, qg, *chunks, up, dmat, rmat)


def norm_kernel(got, h_out, out):
    total = jnp.sum(got[...], axis=0)
    h = total[:, : h_out.shape[1]]
    h_out[...] = h
    tail = total[:, h_out.shape[1] :]
    lane = lax.broadcasted_iota(jnp.int32, tail.shape, 1)
    share = 2.0 / out.shape[0]
    row = jnp.where(lane == 5, jnp.sum(h * h, keepdims=True), tail * share)
    out[...] = jnp.broadcast_to(row[None], out.shape)


def update_kernel(damping, got, h_all, parts, new_solution, new_residual, new_direction, spread):
    total = jnp.sum(got[...], axis=0)
    lane = lax.broadcasted_iota(jnp.int32, total.shape, 1)

    def pick(row, k):
        return jnp.sum(jnp.where(lane == k, row, 0.0), keepdims=True)

    dh, rh, rr, dd, rd, hh = (pick(total, k) for k in range(6))
    damp = damping[0]
    h = h_all[...]
    sol, res, dirn = parts[0:1], parts[1:2], parts[2:3]
    step_len = rr / (dd + dh / damp)
    curved = dirn + h / damp
    rc = rd + rh / damp
    cc = dd + 2.0 * dh / damp + hh / (damp * damp)
    new_norm = rr - 2.0 * step_len * rc + step_len * step_len * cc
    ns = sol + step_len * dirn
    nr = res - step_len * curved
    new_solution[...] = ns
    new_residual[...] = nr
    new_direction[...] = nr + (new_norm / rr) * dirn
    spread[...] = jnp.broadcast_to(ns[None], spread.shape)


def in_vmem(kernel, out_shapes, *args, name, dtype=F32, smem=0):
    return pl.pallas_call(
        kernel,
        out_shape=[jax.ShapeDtypeStruct(s, dtype) for s in out_shapes],
        in_specs=[pl.BlockSpec(memory_space=pltpu.SMEM if i < smem else pltpu.VMEM) for i in range(len(args))],
        out_specs=[pl.BlockSpec(memory_space=pltpu.VMEM)] * len(out_shapes),
        name=name,
    )(*args)


def exchange(x, axes):
    return lax.all_to_all(x, axes, 0, 0, tiled=True)


def spot(yh, z, core, n_z):
    return (yh * n_z + z) * 2 + core


def moves(n_yh, n_z, kinds):
    pairs = []
    for source, target, up in kinds:
        for yh in range(n_yh - up):
            for core in range(2):
                pairs.append((spot(yh, source, core, n_z), spot(yh + up, target, core, n_z)))
    return pairs


def per_device(
    base_queries, adapter_input, adapter_up_weight, projected_keys, projected_values, output_gradient,
    segments, solution, residual, direction, damping,
):
    core, z = lax.axis_index("core"), lax.axis_index("z")
    n_yh, n_z, n_task = lax.axis_size("yh"), lax.axis_size("z"), lax.axis_size("task")
    idx = lax.axis_index(CTX)

    last = n_z - 1
    row = [(i, i + 1, 0) for i in range(last)]

    def move(x, *kinds):
        return lax.ppermute(x, CTX, moves(n_yh, n_z, kinds))

    (own,) = in_vmem(
        pack_kernel, [(BLOCK + SEG_ROWS, 4 * KHALF)], projected_keys[0], projected_values[0], segments, name="pack", dtype=BF16
    )
    (qg,) = in_vmem(
        pack_queries_kernel, [(2, BLOCK, 2 * HALF + 128)], base_queries[0], output_gradient[0], adapter_input[0].T,
        name="pack_queries", dtype=BF16,
    )
    first = move(own, *row, (last, 0, 1))
    cross = move(own, (last - 1, 0, 1), (last - 2, last, 1))
    qg = exchange(qg, "core").reshape(CHUNK, 2 * HALF + 128)
    own = lax.all_gather(own, "core")
    up, dmat, rmat = (x.reshape(RANK, 2 * HALF) for x in (adapter_up_weight, direction, residual))
    size = direction.shape[1] // (n_yh * n_z * 2)
    parts = jnp.concatenate([lax.dynamic_slice_in_dim(x, idx * size, size, 1) for x in (solution, residual, direction)])
    first, own, qg, dmat, rmat, parts = lax.optimization_barrier((first, own, qg, dmat, rmat, parts))
    second = move(first, *row)
    passed = jnp.where((z == 0) | (z == last), cross, second)
    third = move(passed, *row, (last, 0, 0))
    second = jnp.where(z == 0, cross, second)
    chunks = [lax.all_gather(x, "core") for x in (third, second, first)] + [own]

    terms = attend(core.reshape(1), qg, chunks, up, dmat, rmat)

    peers = n_yh * n_z
    h, scalars = in_vmem(
        norm_kernel, [(1, GFEAT), (2 * peers, 1, 128)], exchange(terms.reshape(peers, 1, ROW), ("yh", "z")), name="norm"
    )
    new_solution, new_residual, new_direction, spread = in_vmem(
        update_kernel, [(1, size)] * 3 + [(n_task, 1, size)], damping, exchange(scalars, CTX), h, parts, name="update", smem=1
    )
    meta_gradient = jnp.sum(exchange(spread, "task"), axis=(0, 1)) / n_task
    return new_solution, new_residual, new_direction, meta_gradient


def solution(mesh):
    n_task, n_ctx = mesh.devices.shape
    split = Mesh(mesh.devices.reshape(n_task, n_ctx // 16, 8, 2), ("task",) + CTX)
    tokens = P("task", CTX, None)
    whole = P("task", None)
    in_specs = (tokens, tokens, P("task", None, None), tokens, tokens, tokens, P("task", CTX), whole, whole, whole, P("task"))
    out_specs = (P("task", CTX), P("task", CTX), P("task", CTX), P(CTX))
    return jax.shard_map(per_device, mesh=split, in_specs=in_specs, out_specs=out_specs, check_vma=False)
```

```python
import math

import jax
import jax.numpy as jnp
from jax import lax
from jax.experimental import pallas as pl
from jax.experimental.pallas import tpu as pltpu
from jax.sharding import Mesh
from jax.sharding import PartitionSpec as P

HEAD_DIM = 128
RANK = 16
BLOCK = 128
CHUNK = 2 * BLOCK
SPAN = 3
WINDOW = 7 * BLOCK
GROUPS = 2
PER_GROUP = 4
HALF = GROUPS * PER_GROUP * HEAD_DIM
KHALF = GROUPS * HEAD_DIM
GFEAT = PER_GROUP * HEAD_DIM
ROW = GFEAT + 128
SEG_ROWS = 16
F32 = jnp.float32
BF16 = jnp.bfloat16
CTX = ("yh", "z", "core")
NT = (((1,), (1,)), ((), ()))
NN = (((1,), (0,)), ((), ()))


def dot(a, b, dims=NN):
    return lax.dot_general(a, b, dims, preferred_element_type=F32)


def fold(x):
    return x.reshape(x.shape[0] // 8, 8, x.shape[1])


def pack_kernel(keys, values, seg, out):
    n = keys.shape[1]
    out[:BLOCK, :n] = keys[...]
    out[:BLOCK, n:] = values[...]
    first = lax.broadcasted_iota(jnp.int32, (SEG_ROWS, BLOCK), 0) == 0
    row = jnp.where(first, jnp.broadcast_to(seg[...] + 1, (SEG_ROWS, BLOCK)), 0).astype(F32)
    out[BLOCK:, :BLOCK] = row.astype(BF16)
    out[BLOCK:, BLOCK:] = jnp.zeros((SEG_ROWS, out.shape[1] - BLOCK), BF16)


def pack_queries_kernel(queries, grads, adapter_t, out):
    a = jnp.concatenate([adapter_t[...].astype(F32), jnp.zeros((BLOCK - RANK, BLOCK), F32)], axis=0)
    a = jnp.transpose(a).astype(BF16)
    for core in range(2):
        for i, ref in enumerate((queries, grads)):
            for g in range(GROUPS):
                to, at = i * HALF + g * GFEAT, (g * 2 + core) * GFEAT
                out[core, :, to : to + GFEAT] = ref[:, at : at + GFEAT]
        out[core, :, 2 * HALF :] = a


def attend_kernel(
    core_ref, qg, far, c1, c2, c3, up, dmat, rmat, out, c0, sem, keys, keys_t, vals, qs, ts, at, qaug, s_ref, t_ref, u_ref, c_ref
):
    chunks = (c0, c1, c2, c3)
    core = core_ref[0]
    copy = pltpu.make_async_copy(far, c0, sem)
    copy.start()

    def mine(ref):
        parts = [ref[:, pl.ds(pl.multiple_of((g * 2 + core) * GFEAT, GFEAT), GFEAT)] for g in range(GROUPS)]
        return jnp.concatenate(parts, axis=1)

    a_pad = qg[:, 2 * HALF : 2 * HALF + 128]
    a = a_pad[:, :RANK]
    qs[...] = (qg[:, :HALF].astype(F32) + dot(a, mine(up))).astype(BF16)
    d, r = mine(dmat), mine(rmat)
    d1 = d.astype(BF16)
    rest = d - d1.astype(F32)
    d2 = rest.astype(BF16)
    d3 = (rest - d2.astype(F32)).astype(BF16)
    ts[...] = (dot(a, d1) + dot(a, d2) + dot(a, d3)).astype(BF16)
    at[...] = jnp.transpose(a_pad.astype(F32))[:RANK].astype(BF16)
    lane = lax.broadcasted_iota(jnp.int32, (BLOCK, BLOCK), 1).astype(F32)
    for j in (3, 2, 1, 0):
        c = chunks[j]
        if j == 0:
            copy.wait()
        for half in range(2):
            rows = slice((j * 2 + half) * BLOCK, (j * 2 + half + 1) * BLOCK)
            seg_row = c[half, BLOCK:, :BLOCK].astype(F32)[0:1]
            seg = jnp.transpose(jnp.broadcast_to(seg_row, (BLOCK, BLOCK)))
            hit = seg == lane
            for g in range(GROUPS):
                col = pl.multiple_of((g * 2 + core) * HEAD_DIM, HEAD_DIM)
                k = c[half, :BLOCK, pl.ds(col, HEAD_DIM)]
                keys[g, rows, :HEAD_DIM] = k
                keys[g, rows, HEAD_DIM:] = jnp.where(hit, 1.0, 0.0).astype(BF16)
                keys_t[g, :, rows] = jnp.transpose(k.astype(F32)).astype(BF16)
                vals[g, rows, :] = c[half, :BLOCK, pl.ds(2 * KHALF + col, HEAD_DIM)]
            if j == 3:
                qaug[half] = jnp.where(hit, 0.0, -1e30).astype(BF16)
    tri = jnp.where(lax.broadcasted_iota(jnp.int32, (BLOCK, BLOCK), 0) <= lax.broadcasted_iota(jnp.int32, (BLOCK, BLOCK), 1), 0.0, -1e30)
    cexp = HEAD_DIM**-0.5 * math.log2(math.e)
    steps = [(g, b, pair) for g in range(GROUPS) for b in range(2) for pair in range(2)]

    def scores(n):
        g, b, pair = steps[n]
        slot = n % 3
        win = slice(b * BLOCK, b * BLOCK + WINDOW)
        own = slice(b * BLOCK, (b + 1) * BLOCK)

        def two(ref, base):
            cols = [base + g * GFEAT + (pair * 2 + e) * HEAD_DIM for e in range(2)]
            return [ref[own, col : col + HEAD_DIM] for col in cols]

        q2 = [jnp.concatenate([q, qaug[b]], axis=1) for q in two(qs, 0)]
        q, t, r = (jnp.concatenate(x, axis=0) for x in (q2, two(ts, 0), two(qg, HALF)))

        def do_s():
            s_ref[slot] = dot(keys[g, win, :], q, NT)

        def do_t():
            t_ref[slot] = dot(keys[g, win, :HEAD_DIM], t, NT)

        def do_u():
            u_ref[slot] = dot(vals[g, win, :], r, NT)

        return [do_s, do_t, do_u]

    def weigh(n, ahead):
        slot = n % 3
        scales = []
        for e in range(2):
            lanes = slice(e * BLOCK, (e + 1) * BLOCK)
            m8 = None
            for w in range(6, -1, -1):
                rows = slice(w * BLOCK, (w + 1) * BLOCK)
                s = s_ref[slot, rows, lanes]
                if w == 6:
                    s = s + tri
                top = jnp.max(fold(s), axis=0)
                m8 = top if m8 is None else jnp.maximum(m8, top)
            m = jnp.max(m8, axis=0, keepdims=True)
            if ahead:
                ahead.pop(0)()
            z8 = et8 = eu8 = etu8 = jnp.zeros((8, BLOCK), F32)
            for w in range(7):
                rows = slice(w * BLOCK, (w + 1) * BLOCK)
                s = s_ref[slot, rows, lanes]
                if w == 6:
                    s = s + tri
                ex = jnp.exp2((s - m) * cexp)
                s_ref[slot, rows, lanes] = ex
                et = ex * t_ref[slot, rows, lanes]
                u = u_ref[slot, rows, lanes]
                z8 = z8 + jnp.sum(fold(ex), axis=0)
                et8 = et8 + jnp.sum(fold(et), axis=0)
                eu8 = eu8 + jnp.sum(fold(ex * u), axis=0)
                etu8 = etu8 + jnp.sum(fold(et * u), axis=0)
            inv = 1.0 / jnp.sum(z8, axis=0, keepdims=True)
            mt = jnp.sum(et8, axis=0, keepdims=True) * inv
            mu = jnp.sum(eu8, axis=0, keepdims=True) * inv
            cov = jnp.sum(etu8, axis=0, keepdims=True) * inv - mt * mu
            for w in range(7):
                rows = slice(w * BLOCK, (w + 1) * BLOCK)
                coef = s_ref[slot, rows, lanes] * (
                    (t_ref[slot, rows, lanes] - mt) * (u_ref[slot, rows, lanes] - mu) - cov
                )
                c_ref[slot, rows, lanes] = coef.astype(BF16)
            if ahead:
                ahead.pop(0)()
            scales.append(inv * (1.0 / HEAD_DIM))
        return scales

    def gather(n, scales):
        g, b, pair = steps[n]
        slot = n % 3
        hv = dot(keys_t[g, :, b * BLOCK : b * BLOCK + WINDOW], c_ref[slot])
        ab = at[:, b * BLOCK : (b + 1) * BLOCK]
        for e in range(2):
            lanes = slice(e * BLOCK, (e + 1) * BLOCK)
            head = (hv[:, lanes] * scales[e]).astype(BF16)
            left = g * ROW + (pair * 2 + e) * HEAD_DIM
            cols = slice(left, left + HEAD_DIM)
            part = dot(ab, head, NT)
            if b == 0:
                out[:, cols] = part
            else:
                out[:, cols] += part

    for matmul in scores(0):
        matmul()
    for n in range(8):
        gather(n, weigh(n, scores(n + 1) if n < 7 else []))
    h = jnp.concatenate([out[:, g * ROW : g * ROW + GFEAT] for g in range(GROUPS)], axis=1)
    lane = lax.broadcasted_iota(jnp.int32, (RANK, 128), 1)
    tail = jnp.zeros((RANK, 128), F32)
    share = 1.0 / (RANK * GROUPS)
    for k, term in enumerate((h * d, h * r, r * r * share, d * d * share, r * d * share)):
        tail = jnp.where(lane == k, jnp.sum(term, keepdims=True), tail)
    for g in range(GROUPS):
        out[:, g * ROW + GFEAT : (g + 1) * ROW] = tail


def attend(core, qg, chunks, up, dmat, rmat):
    vm = pltpu.VMEM
    return pl.pallas_call(
        attend_kernel,
        out_shape=jax.ShapeDtypeStruct((RANK, GROUPS * ROW), F32),
        in_specs=[pl.BlockSpec(memory_space=x) for x in (pltpu.SMEM, vm, pl.ANY, vm, vm, vm, vm, vm, vm)],
        out_specs=pl.BlockSpec(memory_space=vm),
        scratch_shapes=[
            vm((2, BLOCK + SEG_ROWS, 4 * KHALF), BF16),
            pltpu.SemaphoreType.DMA,
            vm((GROUPS, 4 * CHUNK, 2 * HEAD_DIM), BF16),
            vm((GROUPS, HEAD_DIM, 4 * CHUNK), BF16),
            vm((GROUPS, 4 * CHUNK, HEAD_DIM), BF16),
            vm((CHUNK, HALF), BF16),
            vm((CHUNK, HALF), BF16),
            vm((RANK, CHUNK), BF16),
            vm((2, BLOCK, BLOCK), BF16),
            vm((3, WINDOW, CHUNK), F32),
            vm((3, WINDOW, CHUNK), F32),
            vm((3, WINDOW, CHUNK), F32),
            vm((3, WINDOW, CHUNK), BF16),
        ],
        compiler_params=pltpu.CompilerParams(vmem_limit_bytes=48 * 1024 * 1024),
        cost_estimate=pl.CostEstimate(flops=2_000_000_000, bytes_accessed=4_000_000, transcendentals=2_000_000),
        name="attend",
    )(core, qg, *chunks, up, dmat, rmat)


def norm_kernel(got, h_out, out):
    total = jnp.sum(got[...], axis=0)
    h = total[:, : h_out.shape[1]]
    h_out[...] = h
    tail = total[:, h_out.shape[1] :]
    lane = lax.broadcasted_iota(jnp.int32, tail.shape, 1)
    share = 2.0 / out.shape[0]
    row = jnp.where(lane == 5, jnp.sum(h * h, keepdims=True), tail * share)
    out[...] = jnp.broadcast_to(row[None], out.shape)


def update_kernel(damping, got, h_all, parts, new_solution, new_residual, new_direction, spread):
    total = jnp.sum(got[...], axis=0)
    lane = lax.broadcasted_iota(jnp.int32, total.shape, 1)

    def pick(row, k):
        return jnp.sum(jnp.where(lane == k, row, 0.0), keepdims=True)

    dh, rh, rr, dd, rd, hh = (pick(total, k) for k in range(6))
    damp = damping[0]
    h = h_all[...]
    sol, res, dirn = parts[0:1], parts[1:2], parts[2:3]
    step_len = rr / (dd + dh / damp)
    curved = dirn + h / damp
    rc = rd + rh / damp
    cc = dd + 2.0 * dh / damp + hh / (damp * damp)
    new_norm = rr - 2.0 * step_len * rc + step_len * step_len * cc
    ns = sol + step_len * dirn
    nr = res - step_len * curved
    new_solution[...] = ns
    new_residual[...] = nr
    new_direction[...] = nr + (new_norm / rr) * dirn
    spread[...] = jnp.broadcast_to(ns[None], spread.shape)


def in_vmem(kernel, out_shapes, *args, name, dtype=F32, smem=0):
    return pl.pallas_call(
        kernel,
        out_shape=[jax.ShapeDtypeStruct(s, dtype) for s in out_shapes],
        in_specs=[pl.BlockSpec(memory_space=pltpu.SMEM if i < smem else pltpu.VMEM) for i in range(len(args))],
        out_specs=[pl.BlockSpec(memory_space=pltpu.VMEM)] * len(out_shapes),
        name=name,
    )(*args)


def exchange(x, axes):
    return lax.all_to_all(x, axes, 0, 0, tiled=True)


def spot(yh, z, core, n_z):
    return (yh * n_z + z) * 2 + core


def moves(n_yh, n_z, kinds):
    pairs = []
    for source, target, up in kinds:
        for yh in range(n_yh - up):
            for core in range(2):
                pairs.append((spot(yh, source, core, n_z), spot(yh + up, target, core, n_z)))
    return pairs


def per_device(
    base_queries, adapter_input, adapter_up_weight, projected_keys, projected_values, output_gradient,
    segments, solution, residual, direction, damping,
):
    core, z = lax.axis_index("core"), lax.axis_index("z")
    n_yh, n_z, n_task = lax.axis_size("yh"), lax.axis_size("z"), lax.axis_size("task")
    idx = lax.axis_index(CTX)

    last = n_z - 1
    row = [(i, i + 1, 0) for i in range(last)]

    def move(x, *kinds):
        return lax.ppermute(x, CTX, moves(n_yh, n_z, kinds))

    (own,) = in_vmem(
        pack_kernel, [(BLOCK + SEG_ROWS, 4 * KHALF)], projected_keys[0], projected_values[0], segments, name="pack", dtype=BF16
    )
    (qg,) = in_vmem(
        pack_queries_kernel, [(2, BLOCK, 2 * HALF + 128)], base_queries[0], output_gradient[0], adapter_input[0].T,
        name="pack_queries", dtype=BF16,
    )
    cross = move(own, (last, 1, 1), (last - 1, 0, 1), (last - 2, 2, 1))
    first = move(own, *row)
    qg = exchange(qg, "core").reshape(CHUNK, 2 * HALF + 128)
    own = lax.all_gather(own, "core")
    up, dmat, rmat = (x.reshape(RANK, 2 * HALF) for x in (adapter_up_weight, direction, residual))
    size = direction.shape[1] // (n_yh * n_z * 2)
    parts = jnp.concatenate([lax.dynamic_slice_in_dim(x, idx * size, size, 1) for x in (solution, residual, direction)])
    first, own, qg, dmat, rmat, parts = lax.optimization_barrier((first, own, qg, dmat, rmat, parts))
    second = jnp.where(z <= 1, cross, move(first, *row[1:]))
    back = move(cross, (1, 0, 0))
    far = move(cross, (2, 0, 0))
    third = jnp.where(z == 0, far, move(second, *row))
    first = jnp.where(z == 0, back, first)
    chunks = [lax.all_gather(x, "core") for x in (third, second, first)] + [own]

    terms = attend(core.reshape(1), qg, chunks, up, dmat, rmat)

    peers = n_yh * n_z
    h, scalars = in_vmem(
        norm_kernel, [(1, GFEAT), (2 * peers, 1, 128)], exchange(terms.reshape(peers, 1, ROW), ("yh", "z")), name="norm"
    )
    new_solution, new_residual, new_direction, spread = in_vmem(
        update_kernel, [(1, size)] * 3 + [(n_task, 1, size)], damping, exchange(scalars, CTX), h, parts, name="update", smem=1
    )
    meta_gradient = jnp.sum(exchange(spread, "task"), axis=(0, 1)) / n_task
    return new_solution, new_residual, new_direction, meta_gradient


def solution(mesh):
    n_task, n_ctx = mesh.devices.shape
    split = Mesh(mesh.devices.reshape(n_task, n_ctx // 16, 8, 2), ("task",) + CTX)
    tokens = P("task", CTX, None)
    whole = P("task", None)
    in_specs = (tokens, tokens, P("task", None, None), tokens, tokens, tokens, P("task", CTX), whole, whole, whole, P("task"))
    out_specs = (P("task", CTX), P("task", CTX), P("task", CTX), P(CTX))
    return jax.shard_map(per_device, mesh=split, in_specs=in_specs, out_specs=out_specs, check_vma=False)
```

```python
import math

import jax
import jax.numpy as jnp
from jax import lax
from jax.experimental import pallas as pl
from jax.experimental.pallas import tpu as pltpu
from jax.sharding import Mesh
from jax.sharding import PartitionSpec as P

HEAD_DIM = 128
RANK = 16
BLOCK = 128
CHUNK = 2 * BLOCK
SPAN = 3
KEYS = (SPAN + 1) * CHUNK
GROUPS = 2
PER_GROUP = 4
HALF = GROUPS * PER_GROUP * HEAD_DIM
KHALF = GROUPS * HEAD_DIM
GFEAT = PER_GROUP * HEAD_DIM
ROW = GFEAT + 128
SEG_ROWS = 16
F32 = jnp.float32
BF16 = jnp.bfloat16
CTX = ("yh", "z", "core")
NT = (((1,), (1,)), ((), ()))
NN = (((1,), (0,)), ((), ()))


def dot(a, b, dims=NN):
    return lax.dot_general(a, b, dims, preferred_element_type=F32)


def fold(x):
    return x.reshape(x.shape[0] // 8, 8, x.shape[1])


def pack_kernel(keys, values, seg, out):
    n = keys.shape[1]
    out[:BLOCK, :n] = keys[...]
    out[:BLOCK, n:] = values[...]
    first = lax.broadcasted_iota(jnp.int32, (SEG_ROWS, BLOCK), 0) == 0
    row = jnp.where(first, jnp.broadcast_to(seg[...] + 1, (SEG_ROWS, BLOCK)), 0).astype(F32)
    out[BLOCK:, :BLOCK] = row.astype(BF16)
    out[BLOCK:, BLOCK:] = jnp.zeros((SEG_ROWS, out.shape[1] - BLOCK), BF16)


def pack_queries_kernel(queries, grads, adapter_t, out):
    a = jnp.concatenate([adapter_t[...].astype(F32), jnp.zeros((BLOCK - RANK, BLOCK), F32)], axis=0)
    a = jnp.transpose(a).astype(BF16)
    for core in range(2):
        for i, ref in enumerate((queries, grads)):
            for g in range(GROUPS):
                to, at = i * HALF + g * GFEAT, (g * 2 + core) * GFEAT
                out[core, :, to : to + GFEAT] = ref[:, at : at + GFEAT]
        out[core, :, 2 * HALF :] = a


def attend_kernel(
    core_ref, qg, far, c1, c2, c3, up, dmat, rmat, out, c0, sem, keys, keys_t, vals, qs, ts, at, qaug, s_ref, t_ref, u_ref, c_ref
):
    chunks = (c0, c1, c2, c3)
    core = core_ref[0]
    copy = pltpu.make_async_copy(far, c0, sem)
    copy.start()

    def mine(ref):
        parts = [ref[:, pl.ds(pl.multiple_of((g * 2 + core) * GFEAT, GFEAT), GFEAT)] for g in range(GROUPS)]
        return jnp.concatenate(parts, axis=1)

    a_pad = qg[:, 2 * HALF : 2 * HALF + 128]
    a = a_pad[:, :RANK]
    qs[...] = (qg[:, :HALF].astype(F32) + dot(a, mine(up))).astype(BF16)
    d, r = mine(dmat), mine(rmat)
    d1 = d.astype(BF16)
    rest = d - d1.astype(F32)
    d2 = rest.astype(BF16)
    d3 = (rest - d2.astype(F32)).astype(BF16)
    ts[...] = (dot(a, d1) + dot(a, d2) + dot(a, d3)).astype(BF16)
    at[...] = jnp.transpose(a_pad.astype(F32))[:RANK].astype(BF16)
    lane = lax.broadcasted_iota(jnp.int32, (BLOCK, BLOCK), 1).astype(F32)
    for j in (3, 2, 1, 0):
        c = chunks[j]
        if j == 0:
            copy.wait()
        for half in range(2):
            rows = slice((j * 2 + half) * BLOCK, (j * 2 + half + 1) * BLOCK)
            seg_row = c[half, BLOCK:, :BLOCK].astype(F32)[0:1]
            seg = jnp.transpose(jnp.broadcast_to(seg_row, (BLOCK, BLOCK)))
            hit = seg == lane
            for g in range(GROUPS):
                col = pl.multiple_of((g * 2 + core) * HEAD_DIM, HEAD_DIM)
                k = c[half, :BLOCK, pl.ds(col, HEAD_DIM)]
                keys[g, rows, :HEAD_DIM] = k
                keys[g, rows, HEAD_DIM:] = jnp.where(hit, 1.0, 0.0).astype(BF16)
                keys_t[g, :, rows] = jnp.transpose(k.astype(F32)).astype(BF16)
                vals[g, rows, :] = c[half, :BLOCK, pl.ds(2 * KHALF + col, HEAD_DIM)]
            if j == 3:
                qaug[half] = jnp.where(hit, 0.0, -1e30).astype(BF16)
    tri = jnp.where(lax.broadcasted_iota(jnp.int32, (BLOCK, BLOCK), 0) <= lax.broadcasted_iota(jnp.int32, (BLOCK, BLOCK), 1), 0.0, -1e30)
    cexp = HEAD_DIM**-0.5 * math.log2(math.e)
    steps = [(g, b, pair) for g in range(GROUPS) for b in range(2) for pair in range(2)]

    def scores(n):
        g, b, pair = steps[n]
        slot = n % 3
        win = slice(0, KEYS - (1 - b) * BLOCK)
        own = slice(b * BLOCK, (b + 1) * BLOCK)

        def two(ref, base):
            cols = [base + g * GFEAT + (pair * 2 + e) * HEAD_DIM for e in range(2)]
            return [ref[own, col : col + HEAD_DIM] for col in cols]

        q2 = [jnp.concatenate([q, qaug[b]], axis=1) for q in two(qs, 0)]
        q, t, r = (jnp.concatenate(x, axis=0) for x in (q2, two(ts, 0), two(qg, HALF)))

        def do_s():
            s_ref[slot, win, :] = dot(keys[g, win, :], q, NT)

        def do_t():
            t_ref[slot, win, :] = dot(keys[g, win, :HEAD_DIM], t, NT)

        def do_u():
            u_ref[slot, win, :] = dot(vals[g, win, :], r, NT)

        return [do_s, do_t, do_u]

    def weigh(n, ahead):
        slot = n % 3
        blocks = 7 + steps[n][1]
        scales = []
        for e in range(2):
            lanes = slice(e * BLOCK, (e + 1) * BLOCK)
            m8 = None
            for w in range(blocks - 1, -1, -1):
                rows = slice(w * BLOCK, (w + 1) * BLOCK)
                s = s_ref[slot, rows, lanes]
                if w == blocks - 1:
                    s = s + tri
                top = jnp.max(fold(s), axis=0)
                m8 = top if m8 is None else jnp.maximum(m8, top)
            m = jnp.max(m8, axis=0, keepdims=True)
            if ahead:
                ahead.pop(0)()
            z8 = et8 = eu8 = etu8 = jnp.zeros((8, BLOCK), F32)
            for w in range(blocks):
                rows = slice(w * BLOCK, (w + 1) * BLOCK)
                s = s_ref[slot, rows, lanes]
                if w == blocks - 1:
                    s = s + tri
                ex = jnp.exp2((s - m) * cexp)
                s_ref[slot, rows, lanes] = ex
                et = ex * t_ref[slot, rows, lanes]
                u = u_ref[slot, rows, lanes]
                z8 = z8 + jnp.sum(fold(ex), axis=0)
                et8 = et8 + jnp.sum(fold(et), axis=0)
                eu8 = eu8 + jnp.sum(fold(ex * u), axis=0)
                etu8 = etu8 + jnp.sum(fold(et * u), axis=0)
            inv = 1.0 / jnp.sum(z8, axis=0, keepdims=True)
            mt = jnp.sum(et8, axis=0, keepdims=True) * inv
            mu = jnp.sum(eu8, axis=0, keepdims=True) * inv
            cov = jnp.sum(etu8, axis=0, keepdims=True) * inv - mt * mu
            for w in range(blocks):
                rows = slice(w * BLOCK, (w + 1) * BLOCK)
                coef = s_ref[slot, rows, lanes] * (
                    (t_ref[slot, rows, lanes] - mt) * (u_ref[slot, rows, lanes] - mu) - cov
                )
                c_ref[slot, rows, lanes] = coef.astype(BF16)
            if ahead:
                ahead.pop(0)()
            scales.append(inv * (1.0 / HEAD_DIM))
        return scales

    def gather(n, scales):
        g, b, pair = steps[n]
        slot = n % 3
        win = slice(0, KEYS - (1 - b) * BLOCK)
        hv = dot(keys_t[g, :, win], c_ref[slot, win, :])
        ab = at[:, b * BLOCK : (b + 1) * BLOCK]
        for e in range(2):
            lanes = slice(e * BLOCK, (e + 1) * BLOCK)
            head = (hv[:, lanes] * scales[e]).astype(BF16)
            left = g * ROW + (pair * 2 + e) * HEAD_DIM
            cols = slice(left, left + HEAD_DIM)
            part = dot(ab, head, NT)
            if b == 0:
                out[:, cols] = part
            else:
                out[:, cols] += part

    for matmul in scores(0):
        matmul()
    for n in range(8):
        gather(n, weigh(n, scores(n + 1) if n < 7 else []))
    h = jnp.concatenate([out[:, g * ROW : g * ROW + GFEAT] for g in range(GROUPS)], axis=1)
    lane = lax.broadcasted_iota(jnp.int32, (RANK, 128), 1)
    tail = jnp.zeros((RANK, 128), F32)
    share = 1.0 / (RANK * GROUPS)
    for k, term in enumerate((h * d, h * r, r * r * share, d * d * share, r * d * share)):
        tail = jnp.where(lane == k, jnp.sum(term, keepdims=True), tail)
    for g in range(GROUPS):
        out[:, g * ROW + GFEAT : (g + 1) * ROW] = tail


def attend(core, qg, chunks, up, dmat, rmat):
    vm = pltpu.VMEM
    return pl.pallas_call(
        attend_kernel,
        out_shape=jax.ShapeDtypeStruct((RANK, GROUPS * ROW), F32),
        in_specs=[pl.BlockSpec(memory_space=x) for x in (pltpu.SMEM, vm, pl.ANY, vm, vm, vm, vm, vm, vm)],
        out_specs=pl.BlockSpec(memory_space=vm),
        scratch_shapes=[
            vm((2, BLOCK + SEG_ROWS, 4 * KHALF), BF16),
            pltpu.SemaphoreType.DMA,
            vm((GROUPS, 4 * CHUNK, 2 * HEAD_DIM), BF16),
            vm((GROUPS, HEAD_DIM, 4 * CHUNK), BF16),
            vm((GROUPS, 4 * CHUNK, HEAD_DIM), BF16),
            vm((CHUNK, HALF), BF16),
            vm((CHUNK, HALF), BF16),
            vm((RANK, CHUNK), BF16),
            vm((2, BLOCK, BLOCK), BF16),
            vm((3, KEYS, CHUNK), F32),
            vm((3, KEYS, CHUNK), F32),
            vm((3, KEYS, CHUNK), F32),
            vm((3, KEYS, CHUNK), BF16),
        ],
        compiler_params=pltpu.CompilerParams(vmem_limit_bytes=48 * 1024 * 1024),
        cost_estimate=pl.CostEstimate(flops=2_000_000_000, bytes_accessed=4_000_000, transcendentals=2_000_000),
        name="attend",
    )(core, qg, *chunks, up, dmat, rmat)


def norm_kernel(got, h_out, out):
    total = jnp.sum(got[...], axis=0)
    h = total[:, : h_out.shape[1]]
    h_out[...] = h
    tail = total[:, h_out.shape[1] :]
    lane = lax.broadcasted_iota(jnp.int32, tail.shape, 1)
    share = 2.0 / out.shape[0]
    row = jnp.where(lane == 5, jnp.sum(h * h, keepdims=True), tail * share)
    out[...] = jnp.broadcast_to(row[None], out.shape)


def update_kernel(damping, got, h_all, parts, new_solution, new_residual, new_direction, spread):
    total = jnp.sum(got[...], axis=0)
    lane = lax.broadcasted_iota(jnp.int32, total.shape, 1)

    def pick(row, k):
        return jnp.sum(jnp.where(lane == k, row, 0.0), keepdims=True)

    dh, rh, rr, dd, rd, hh = (pick(total, k) for k in range(6))
    damp = damping[0]
    h = h_all[...]
    sol, res, dirn = parts[0:1], parts[1:2], parts[2:3]
    step_len = rr / (dd + dh / damp)
    curved = dirn + h / damp
    rc = rd + rh / damp
    cc = dd + 2.0 * dh / damp + hh / (damp * damp)
    new_norm = rr - 2.0 * step_len * rc + step_len * step_len * cc
    ns = sol + step_len * dirn
    nr = res - step_len * curved
    new_solution[...] = ns
    new_residual[...] = nr
    new_direction[...] = nr + (new_norm / rr) * dirn
    spread[...] = jnp.broadcast_to(ns[None], spread.shape)


def in_vmem(kernel, out_shapes, *args, name, dtype=F32, smem=0):
    return pl.pallas_call(
        kernel,
        out_shape=[jax.ShapeDtypeStruct(s, dtype) for s in out_shapes],
        in_specs=[pl.BlockSpec(memory_space=pltpu.SMEM if i < smem else pltpu.VMEM) for i in range(len(args))],
        out_specs=[pl.BlockSpec(memory_space=pltpu.VMEM)] * len(out_shapes),
        name=name,
    )(*args)


def exchange(x, axes):
    return lax.all_to_all(x, axes, 0, 0, tiled=True)


def spot(yh, z, core, n_z):
    return (yh * n_z + z) * 2 + core


def moves(n_yh, n_z, kinds):
    pairs = []
    for source, target, up in kinds:
        for yh in range(n_yh - up):
            for core in range(2):
                pairs.append((spot(yh, source, core, n_z), spot(yh + up, target, core, n_z)))
    return pairs


def per_device(
    base_queries, adapter_input, adapter_up_weight, projected_keys, projected_values, output_gradient,
    segments, solution, residual, direction, damping,
):
    core, z = lax.axis_index("core"), lax.axis_index("z")
    n_yh, n_z, n_task = lax.axis_size("yh"), lax.axis_size("z"), lax.axis_size("task")
    idx = lax.axis_index(CTX)

    last = n_z - 1
    row = [(i, i + 1, 0) for i in range(last)]

    def move(x, *kinds):
        return lax.ppermute(x, CTX, moves(n_yh, n_z, kinds))

    (own,) = in_vmem(
        pack_kernel, [(BLOCK + SEG_ROWS, 4 * KHALF)], projected_keys[0], projected_values[0], segments, name="pack", dtype=BF16
    )
    (qg,) = in_vmem(
        pack_queries_kernel, [(2, BLOCK, 2 * HALF + 128)], base_queries[0], output_gradient[0], adapter_input[0].T,
        name="pack_queries", dtype=BF16,
    )
    cross = move(own, (last, 1, 1), (last - 1, 0, 1), (last - 2, 2, 1))
    first = move(own, *row)
    qg = exchange(qg, "core").reshape(CHUNK, 2 * HALF + 128)
    own = lax.all_gather(own, "core")
    up, dmat, rmat = (x.reshape(RANK, 2 * HALF) for x in (adapter_up_weight, direction, residual))
    size = direction.shape[1] // (n_yh * n_z * 2)
    parts = jnp.concatenate([lax.dynamic_slice_in_dim(x, idx * size, size, 1) for x in (solution, residual, direction)])
    first, own, qg, dmat, rmat, parts = lax.optimization_barrier((first, own, qg, dmat, rmat, parts))
    second = jnp.where(z <= 1, cross, move(first, *row[1:]))
    back = move(cross, (1, 0, 0))
    far = move(cross, (2, 0, 0))
    third = move(second, *row)
    chunks = [jnp.where(z == 0, back, third), second, jnp.where(z == 0, far, first)]
    chunks = [lax.all_gather(x, "core") for x in chunks] + [own]

    terms = attend(core.reshape(1), qg, chunks, up, dmat, rmat)

    peers = n_yh * n_z
    h, scalars = in_vmem(
        norm_kernel, [(1, GFEAT), (2 * peers, 1, 128)], exchange(terms.reshape(peers, 1, ROW), ("yh", "z")), name="norm"
    )
    new_solution, new_residual, new_direction, spread = in_vmem(
        update_kernel, [(1, size)] * 3 + [(n_task, 1, size)], damping, exchange(scalars, CTX), h, parts, name="update", smem=1
    )
    meta_gradient = jnp.sum(exchange(spread, "task"), axis=(0, 1)) / n_task
    return new_solution, new_residual, new_direction, meta_gradient


def solution(mesh):
    n_task, n_ctx = mesh.devices.shape
    split = Mesh(mesh.devices.reshape(n_task, n_ctx // 16, 8, 2), ("task",) + CTX)
    tokens = P("task", CTX, None)
    whole = P("task", None)
    in_specs = (tokens, tokens, P("task", None, None), tokens, tokens, tokens, P("task", CTX), whole, whole, whole, P("task"))
    out_specs = (P("task", CTX), P("task", CTX), P("task", CTX), P(CTX))
    return jax.shard_map(per_device, mesh=split, in_specs=in_specs, out_specs=out_specs, check_vma=False)
```

```python
import math

import jax
import jax.numpy as jnp
from jax import lax
from jax.experimental import pallas as pl
from jax.experimental.pallas import tpu as pltpu
from jax.sharding import Mesh
from jax.sharding import PartitionSpec as P

HEAD_DIM = 128
RANK = 16
BLOCK = 128
CHUNK = 2 * BLOCK
SPAN = 3
KEYS = (SPAN + 1) * CHUNK
GROUPS = 2
PER_GROUP = 4
HALF = GROUPS * PER_GROUP * HEAD_DIM
KHALF = GROUPS * HEAD_DIM
GFEAT = PER_GROUP * HEAD_DIM
ROW = GFEAT + 128
SEG_ROWS = 16
F32 = jnp.float32
BF16 = jnp.bfloat16
CTX = ("yh", "z", "core")
NT = (((1,), (1,)), ((), ()))
NN = (((1,), (0,)), ((), ()))


def dot(a, b, dims=NN):
    return lax.dot_general(a, b, dims, preferred_element_type=F32)


def fold(x):
    return x.reshape(x.shape[0] // 8, 8, x.shape[1])


def pack_kernel(keys, values, seg, out):
    n = keys.shape[1]
    out[:BLOCK, :n] = keys[...]
    out[:BLOCK, n:] = values[...]
    first = lax.broadcasted_iota(jnp.int32, (SEG_ROWS, BLOCK), 0) == 0
    row = jnp.where(first, jnp.broadcast_to(seg[...] + 1, (SEG_ROWS, BLOCK)), 0).astype(F32)
    out[BLOCK:, :BLOCK] = row.astype(BF16)
    out[BLOCK:, BLOCK:] = jnp.zeros((SEG_ROWS, out.shape[1] - BLOCK), BF16)


def pack_queries_kernel(queries, grads, adapter_t, out):
    a = jnp.concatenate([adapter_t[...].astype(F32), jnp.zeros((BLOCK - RANK, BLOCK), F32)], axis=0)
    a = jnp.transpose(a).astype(BF16)
    for core in range(2):
        for i, ref in enumerate((queries, grads)):
            for g in range(GROUPS):
                to, at = i * HALF + g * GFEAT, (g * 2 + core) * GFEAT
                out[core, :, to : to + GFEAT] = ref[:, at : at + GFEAT]
        out[core, :, 2 * HALF :] = a


def attend_kernel(
    core_ref, qg, far, c1, c2, c3, up, dmat, rmat, out, c0, sem, keys, keys_t, vals, qs, ts, at, qaug, s_ref, t_ref, u_ref, c_ref
):
    chunks = (c0, c1, c2, c3)
    core = core_ref[0]
    copy = pltpu.make_async_copy(far, c0, sem)
    copy.start()

    def mine(ref):
        parts = [ref[:, pl.ds(pl.multiple_of((g * 2 + core) * GFEAT, GFEAT), GFEAT)] for g in range(GROUPS)]
        return jnp.concatenate(parts, axis=1)

    a_pad = qg[:, 2 * HALF : 2 * HALF + 128]
    a = a_pad[:, :RANK]
    qs[...] = (qg[:, :HALF].astype(F32) + dot(a, mine(up))).astype(BF16)
    d, r = mine(dmat), mine(rmat)
    d1 = d.astype(BF16)
    rest = d - d1.astype(F32)
    d2 = rest.astype(BF16)
    d3 = (rest - d2.astype(F32)).astype(BF16)
    ts[...] = (dot(a, d1) + dot(a, d2) + dot(a, d3)).astype(BF16)
    at[...] = jnp.transpose(a_pad.astype(F32))[:RANK].astype(BF16)
    lane = lax.broadcasted_iota(jnp.int32, (BLOCK, BLOCK), 1).astype(F32)
    for j in (3, 2, 1, 0):
        c = chunks[j]
        if j == 0:
            copy.wait()
        for half in range(2):
            rows = slice((j * 2 + half) * BLOCK, (j * 2 + half + 1) * BLOCK)
            seg_row = c[half, BLOCK:, :BLOCK].astype(F32)[0:1]
            seg = jnp.transpose(jnp.broadcast_to(seg_row, (BLOCK, BLOCK)))
            hit = seg == lane
            for g in range(GROUPS):
                col = pl.multiple_of((g * 2 + core) * HEAD_DIM, HEAD_DIM)
                k = c[half, :BLOCK, pl.ds(col, HEAD_DIM)]
                keys[g, rows, :HEAD_DIM] = k
                keys[g, rows, HEAD_DIM:] = jnp.where(hit, 1.0, 0.0).astype(BF16)
                keys_t[g, :, rows] = jnp.transpose(k.astype(F32)).astype(BF16)
                vals[g, rows, :] = c[half, :BLOCK, pl.ds(2 * KHALF + col, HEAD_DIM)]
            if j == 3:
                qaug[half] = jnp.where(hit, 0.0, -1e30).astype(BF16)
    tri = jnp.where(lax.broadcasted_iota(jnp.int32, (BLOCK, BLOCK), 0) <= lax.broadcasted_iota(jnp.int32, (BLOCK, BLOCK), 1), 0.0, -1e30)
    cexp = HEAD_DIM**-0.5 * math.log2(math.e)
    steps = [(g, b, pair) for g in range(GROUPS) for b in range(2) for pair in range(2)]

    def scores(n):
        g, b, pair = steps[n]
        slot = n % 3
        win = slice(0, KEYS - (1 - b) * BLOCK)
        own = slice(b * BLOCK, (b + 1) * BLOCK)

        def two(ref, base):
            cols = [base + g * GFEAT + (pair * 2 + e) * HEAD_DIM for e in range(2)]
            return [ref[own, col : col + HEAD_DIM] for col in cols]

        q2 = [jnp.concatenate([q, qaug[b]], axis=1) for q in two(qs, 0)]
        q, t, r = (jnp.concatenate(x, axis=0) for x in (q2, two(ts, 0), two(qg, HALF)))

        def do_s():
            s_ref[slot, win, :] = dot(keys[g, win, :], q, NT)

        def do_t():
            t_ref[slot, win, :] = dot(keys[g, win, :HEAD_DIM], t, NT)

        def do_u():
            u_ref[slot, win, :] = dot(vals[g, win, :], r, NT)

        return [do_s, do_t, do_u]

    def weigh(n, ahead):
        slot = n % 3
        blocks = 7 + steps[n][1]
        scales = []
        for e in range(2):
            lanes = slice(e * BLOCK, (e + 1) * BLOCK)
            m8 = None
            for w in range(blocks - 1, -1, -1):
                rows = slice(w * BLOCK, (w + 1) * BLOCK)
                s = s_ref[slot, rows, lanes]
                if w == blocks - 1:
                    s = s + tri
                top = jnp.max(fold(s), axis=0)
                m8 = top if m8 is None else jnp.maximum(m8, top)
            m = jnp.max(m8, axis=0, keepdims=True)
            if ahead:
                ahead.pop(0)()
            z8 = et8 = eu8 = etu8 = jnp.zeros((8, BLOCK), F32)
            for w in range(blocks):
                rows = slice(w * BLOCK, (w + 1) * BLOCK)
                s = s_ref[slot, rows, lanes]
                if w == blocks - 1:
                    s = s + tri
                ex = jnp.exp2((s - m) * cexp)
                s_ref[slot, rows, lanes] = ex
                et = ex * t_ref[slot, rows, lanes]
                u = u_ref[slot, rows, lanes]
                z8 = z8 + jnp.sum(fold(ex), axis=0)
                et8 = et8 + jnp.sum(fold(et), axis=0)
                eu8 = eu8 + jnp.sum(fold(ex * u), axis=0)
                etu8 = etu8 + jnp.sum(fold(et * u), axis=0)
            inv = 1.0 / jnp.sum(z8, axis=0, keepdims=True)
            mt = jnp.sum(et8, axis=0, keepdims=True) * inv
            mu = jnp.sum(eu8, axis=0, keepdims=True) * inv
            cov = jnp.sum(etu8, axis=0, keepdims=True) * inv - mt * mu
            for w in range(blocks):
                rows = slice(w * BLOCK, (w + 1) * BLOCK)
                coef = s_ref[slot, rows, lanes] * (
                    (t_ref[slot, rows, lanes] - mt) * (u_ref[slot, rows, lanes] - mu) - cov
                )
                c_ref[slot, rows, lanes] = coef.astype(BF16)
            if ahead:
                ahead.pop(0)()
            scales.append(inv * (1.0 / HEAD_DIM))
        return scales

    def gather(n, scales):
        g, b, pair = steps[n]
        slot = n % 3
        win = slice(0, KEYS - (1 - b) * BLOCK)
        hv = dot(keys_t[g, :, win], c_ref[slot, win, :])
        ab = at[:, b * BLOCK : (b + 1) * BLOCK]
        for e in range(2):
            lanes = slice(e * BLOCK, (e + 1) * BLOCK)
            head = (hv[:, lanes] * scales[e]).astype(BF16)
            left = g * ROW + (pair * 2 + e) * HEAD_DIM
            cols = slice(left, left + HEAD_DIM)
            part = dot(ab, head, NT)
            if b == 0:
                out[:, cols] = part
            else:
                out[:, cols] += part

    for matmul in scores(0):
        matmul()
    for n in range(8):
        gather(n, weigh(n, scores(n + 1) if n < 7 else []))
    h = jnp.concatenate([out[:, g * ROW : g * ROW + GFEAT] for g in range(GROUPS)], axis=1)
    lane = lax.broadcasted_iota(jnp.int32, (RANK, 128), 1)
    tail = jnp.zeros((RANK, 128), F32)
    share = 1.0 / (RANK * GROUPS)
    for k, term in enumerate((h * d, h * r, r * r * share, d * d * share, r * d * share)):
        tail = jnp.where(lane == k, jnp.sum(term, keepdims=True), tail)
    for g in range(GROUPS):
        out[:, g * ROW + GFEAT : (g + 1) * ROW] = tail


def attend(core, qg, chunks, up, dmat, rmat):
    vm = pltpu.VMEM
    return pl.pallas_call(
        attend_kernel,
        out_shape=jax.ShapeDtypeStruct((RANK, GROUPS * ROW), F32),
        in_specs=[pl.BlockSpec(memory_space=x) for x in (pltpu.SMEM, vm, pl.ANY, vm, vm, vm, vm, vm, vm)],
        out_specs=pl.BlockSpec(memory_space=vm),
        scratch_shapes=[
            vm((2, BLOCK + SEG_ROWS, 4 * KHALF), BF16),
            pltpu.SemaphoreType.DMA,
            vm((GROUPS, 4 * CHUNK, 2 * HEAD_DIM), BF16),
            vm((GROUPS, HEAD_DIM, 4 * CHUNK), BF16),
            vm((GROUPS, 4 * CHUNK, HEAD_DIM), BF16),
            vm((CHUNK, HALF), BF16),
            vm((CHUNK, HALF), BF16),
            vm((RANK, CHUNK), BF16),
            vm((2, BLOCK, BLOCK), BF16),
            vm((3, KEYS, CHUNK), F32),
            vm((3, KEYS, CHUNK), F32),
            vm((3, KEYS, CHUNK), F32),
            vm((3, KEYS, CHUNK), BF16),
        ],
        compiler_params=pltpu.CompilerParams(vmem_limit_bytes=48 * 1024 * 1024),
        cost_estimate=pl.CostEstimate(flops=2_000_000_000, bytes_accessed=4_000_000, transcendentals=2_000_000),
        name="attend",
    )(core, qg, *chunks, up, dmat, rmat)


def norm_kernel(got, h_out, out):
    total = jnp.sum(got[...], axis=0)
    h = total[:, : h_out.shape[1]]
    h_out[...] = h
    tail = total[:, h_out.shape[1] :]
    lane = lax.broadcasted_iota(jnp.int32, tail.shape, 1)
    share = 2.0 / out.shape[0]
    row = jnp.where(lane == 5, jnp.sum(h * h, keepdims=True), tail * share)
    out[...] = jnp.broadcast_to(row[None], out.shape)


def update_kernel(damping, got, h_all, parts, new_solution, new_residual, new_direction, spread):
    total = jnp.sum(got[...], axis=0)
    lane = lax.broadcasted_iota(jnp.int32, total.shape, 1)

    def pick(row, k):
        return jnp.sum(jnp.where(lane == k, row, 0.0), keepdims=True)

    dh, rh, rr, dd, rd, hh = (pick(total, k) for k in range(6))
    damp = damping[0]
    h = h_all[...]
    sol, res, dirn = parts[0:1], parts[1:2], parts[2:3]
    step_len = rr / (dd + dh / damp)
    curved = dirn + h / damp
    rc = rd + rh / damp
    cc = dd + 2.0 * dh / damp + hh / (damp * damp)
    new_norm = rr - 2.0 * step_len * rc + step_len * step_len * cc
    ns = sol + step_len * dirn
    nr = res - step_len * curved
    new_solution[...] = ns
    new_residual[...] = nr
    new_direction[...] = nr + (new_norm / rr) * dirn
    spread[...] = jnp.broadcast_to(ns[None], spread.shape)


def in_vmem(kernel, out_shapes, *args, name, dtype=F32, smem=0):
    return pl.pallas_call(
        kernel,
        out_shape=[jax.ShapeDtypeStruct(s, dtype) for s in out_shapes],
        in_specs=[pl.BlockSpec(memory_space=pltpu.SMEM if i < smem else pltpu.VMEM) for i in range(len(args))],
        out_specs=[pl.BlockSpec(memory_space=pltpu.VMEM)] * len(out_shapes),
        name=name,
    )(*args)


def exchange(x, axes):
    return lax.all_to_all(x, axes, 0, 0, tiled=True)


def spot(yh, z, core, n_z):
    return (yh * n_z + z) * 2 + core


def moves(n_yh, n_z, kinds):
    pairs = []
    for source, target, up in kinds:
        for yh in range(n_yh - up):
            for core in range(2):
                pairs.append((spot(yh, source, core, n_z), spot(yh + up, target, core, n_z)))
    return pairs


def per_device(
    base_queries, adapter_input, adapter_up_weight, projected_keys, projected_values, output_gradient,
    segments, solution, residual, direction, damping,
):
    core, z = lax.axis_index("core"), lax.axis_index("z")
    n_yh, n_z, n_task = lax.axis_size("yh"), lax.axis_size("z"), lax.axis_size("task")
    idx = lax.axis_index(CTX)

    last = n_z - 1
    row = [(i, i + 1, 0) for i in range(last)]

    def move(x, *kinds):
        return lax.ppermute(x, CTX, moves(n_yh, n_z, kinds))

    (own,) = in_vmem(
        pack_kernel, [(BLOCK + SEG_ROWS, 4 * KHALF)], projected_keys[0], projected_values[0], segments, name="pack", dtype=BF16
    )
    (qg,) = in_vmem(
        pack_queries_kernel, [(2, BLOCK, 2 * HALF + 128)], base_queries[0], output_gradient[0], adapter_input[0].T,
        name="pack_queries", dtype=BF16,
    )
    cross = move(own, (last, 1, 1), (last - 1, 0, 1), (last - 2, 2, 1))
    first = move(own, *row)
    qg = exchange(qg, "core").reshape(CHUNK, 2 * HALF + 128)
    own = lax.all_gather(own, "core")
    up, dmat, rmat = (x.reshape(RANK, 2 * HALF) for x in (adapter_up_weight, direction, residual))
    size = direction.shape[1] // (n_yh * n_z * 2)
    parts = jnp.concatenate([lax.dynamic_slice_in_dim(x, idx * size, size, 1) for x in (solution, residual, direction)])
    first, qg = lax.optimization_barrier((first, qg))
    second = move(first, *row[1:])
    cross, own, dmat, rmat, parts = lax.optimization_barrier((cross, own, dmat, rmat, parts))
    second = jnp.where(z <= 1, cross, second)
    back = move(cross, (1, 0, 0))
    far = move(cross, (2, 0, 0))
    third = move(second, *row)
    second = lax.all_gather(second, "core")
    second, far, first = lax.optimization_barrier((second, far, first))
    first = lax.all_gather(jnp.where(z == 0, far, first), "core")
    chunks = [lax.all_gather(jnp.where(z == 0, back, third), "core"), second, first, own]

    terms = attend(core.reshape(1), qg, chunks, up, dmat, rmat)

    peers = n_yh * n_z
    h, scalars = in_vmem(
        norm_kernel, [(1, GFEAT), (2 * peers, 1, 128)], exchange(terms.reshape(peers, 1, ROW), ("yh", "z")), name="norm"
    )
    new_solution, new_residual, new_direction, spread = in_vmem(
        update_kernel, [(1, size)] * 3 + [(n_task, 1, size)], damping, exchange(scalars, CTX), h, parts, name="update", smem=1
    )
    meta_gradient = jnp.sum(exchange(spread, "task"), axis=(0, 1)) / n_task
    return new_solution, new_residual, new_direction, meta_gradient


def solution(mesh):
    n_task, n_ctx = mesh.devices.shape
    split = Mesh(mesh.devices.reshape(n_task, n_ctx // 16, 8, 2), ("task",) + CTX)
    tokens = P("task", CTX, None)
    whole = P("task", None)
    in_specs = (tokens, tokens, P("task", None, None), tokens, tokens, tokens, P("task", CTX), whole, whole, whole, P("task"))
    out_specs = (P("task", CTX), P("task", CTX), P("task", CTX), P(CTX))
    return jax.shard_map(per_device, mesh=split, in_specs=in_specs, out_specs=out_specs, check_vma=False)
```

```python
import math

import jax
import jax.numpy as jnp
from jax import lax
from jax.experimental import pallas as pl
from jax.experimental.pallas import tpu as pltpu
from jax.sharding import Mesh
from jax.sharding import PartitionSpec as P

HEAD_DIM = 128
RANK = 16
BLOCK = 128
CHUNK = 2 * BLOCK
SPAN = 3
KEYS = (SPAN + 1) * CHUNK
GROUPS = 2
PER_GROUP = 4
HALF = GROUPS * PER_GROUP * HEAD_DIM
KHALF = GROUPS * HEAD_DIM
GFEAT = PER_GROUP * HEAD_DIM
ROW = GFEAT + 128
SEG_ROWS = 16
F32 = jnp.float32
BF16 = jnp.bfloat16
CTX = ("yh", "z", "core")
NT = (((1,), (1,)), ((), ()))
NN = (((1,), (0,)), ((), ()))


def dot(a, b, dims=NN):
    return lax.dot_general(a, b, dims, preferred_element_type=F32)


def fold(x):
    return x.reshape(x.shape[0] // 8, 8, x.shape[1])


def pack_kernel(keys, values, seg, out):
    n = keys.shape[1]
    out[:BLOCK, :n] = keys[...]
    out[:BLOCK, n:] = values[...]
    first = lax.broadcasted_iota(jnp.int32, (SEG_ROWS, BLOCK), 0) == 0
    row = jnp.where(first, jnp.broadcast_to(seg[...] + 1, (SEG_ROWS, BLOCK)), 0).astype(F32)
    out[BLOCK:, :BLOCK] = row.astype(BF16)
    out[BLOCK:, BLOCK:] = jnp.zeros((SEG_ROWS, out.shape[1] - BLOCK), BF16)


def pack_queries_kernel(queries, grads, adapter_t, out):
    a = jnp.concatenate([adapter_t[...].astype(F32), jnp.zeros((BLOCK - RANK, BLOCK), F32)], axis=0)
    a = jnp.transpose(a).astype(BF16)
    for core in range(2):
        for i, ref in enumerate((queries, grads)):
            for g in range(GROUPS):
                to, at = i * HALF + g * GFEAT, (g * 2 + core) * GFEAT
                out[core, :, to : to + GFEAT] = ref[:, at : at + GFEAT]
        out[core, :, 2 * HALF :] = a


def mine(ref, core):
    parts = [ref[:, pl.ds(pl.multiple_of((g * 2 + core) * GFEAT, GFEAT), GFEAT)] for g in range(GROUPS)]
    return jnp.concatenate(parts, axis=1)


def place_keys(c, at_row, core, keys, keys_t, vals):
    lane = lax.broadcasted_iota(jnp.int32, (BLOCK, BLOCK), 1).astype(F32)
    hits = []
    for half in range(2):
        rows = slice(at_row + half * BLOCK, at_row + (half + 1) * BLOCK)
        seg_row = c[half, BLOCK:, :BLOCK].astype(F32)[0:1]
        hit = jnp.transpose(jnp.broadcast_to(seg_row, (BLOCK, BLOCK))) == lane
        hits.append(hit)
        for g in range(GROUPS):
            col = pl.multiple_of((g * 2 + core) * HEAD_DIM, HEAD_DIM)
            k = c[half, :BLOCK, pl.ds(col, HEAD_DIM)]
            keys[g, rows, :HEAD_DIM] = k
            keys[g, rows, HEAD_DIM:] = jnp.where(hit, 1.0, 0.0).astype(BF16)
            keys_t[g, :, rows] = jnp.transpose(k.astype(F32)).astype(BF16)
            vals[g, rows, :] = c[half, :BLOCK, pl.ds(2 * KHALF + col, HEAD_DIM)]
    return hits


def prepare_kernel(core_ref, qg, c1, c2, c3, up, dmat, qs, ts, at, qaug, keys, keys_t, vals):
    core = core_ref[0]
    a_pad = qg[:, 2 * HALF : 2 * HALF + 128]
    a = a_pad[:, :RANK]
    qs[...] = (qg[:, :HALF].astype(F32) + dot(a, mine(up, core))).astype(BF16)
    d = mine(dmat, core)
    d1 = d.astype(BF16)
    rest = d - d1.astype(F32)
    d2 = rest.astype(BF16)
    d3 = (rest - d2.astype(F32)).astype(BF16)
    ts[...] = (dot(a, d1) + dot(a, d2) + dot(a, d3)).astype(BF16)
    at[...] = jnp.transpose(a_pad.astype(F32))[:RANK].astype(BF16)
    for j, c in enumerate((c1, c2, c3)):
        hits = place_keys(c, j * CHUNK, core, keys, keys_t, vals)
    for half in range(2):
        qaug[half] = jnp.where(hits[half], 0.0, -1e30).astype(BF16)


def attend_kernel(
    core_ref, qg, far, qs, ts, at, qaug, near, near_t, near_vals, dmat, rmat,
    out, c0, sem, keys, keys_t, vals, s_ref, t_ref, u_ref, c_ref,
):
    core = core_ref[0]
    copy = pltpu.make_async_copy(far, c0, sem)
    copy.start()
    d, r = mine(dmat, core), mine(rmat, core)
    for g in range(GROUPS):
        keys[g, CHUNK:, :] = near[g]
        keys_t[g, :, CHUNK:] = near_t[g]
        vals[g, CHUNK:, :] = near_vals[g]
    copy.wait()
    place_keys(c0, 0, core, keys, keys_t, vals)
    tri = jnp.where(lax.broadcasted_iota(jnp.int32, (BLOCK, BLOCK), 0) <= lax.broadcasted_iota(jnp.int32, (BLOCK, BLOCK), 1), 0.0, -1e30)
    cexp = HEAD_DIM**-0.5 * math.log2(math.e)
    steps = [(g, b, pair) for g in range(GROUPS) for b in range(2) for pair in range(2)]

    def scores(n):
        g, b, pair = steps[n]
        slot = n % 3
        win = slice(0, KEYS - (1 - b) * BLOCK)
        own = slice(b * BLOCK, (b + 1) * BLOCK)

        def two(ref, base):
            cols = [base + g * GFEAT + (pair * 2 + e) * HEAD_DIM for e in range(2)]
            return [ref[own, col : col + HEAD_DIM] for col in cols]

        q2 = [jnp.concatenate([q, qaug[b]], axis=1) for q in two(qs, 0)]
        q, t, r = (jnp.concatenate(x, axis=0) for x in (q2, two(ts, 0), two(qg, HALF)))

        def do_s():
            s_ref[slot, win, :] = dot(keys[g, win, :], q, NT)

        def do_t():
            t_ref[slot, win, :] = dot(keys[g, win, :HEAD_DIM], t, NT)

        def do_u():
            u_ref[slot, win, :] = dot(vals[g, win, :], r, NT)

        return [do_s, do_t, do_u]

    def weigh(n, ahead):
        slot = n % 3
        blocks = 7 + steps[n][1]
        scales = []
        for e in range(2):
            lanes = slice(e * BLOCK, (e + 1) * BLOCK)
            m8 = None
            for w in range(blocks - 1, -1, -1):
                rows = slice(w * BLOCK, (w + 1) * BLOCK)
                s = s_ref[slot, rows, lanes]
                if w == blocks - 1:
                    s = s + tri
                top = jnp.max(fold(s), axis=0)
                m8 = top if m8 is None else jnp.maximum(m8, top)
            m = jnp.max(m8, axis=0, keepdims=True)
            if ahead:
                ahead.pop(0)()
            z8 = et8 = eu8 = etu8 = jnp.zeros((8, BLOCK), F32)
            for w in range(blocks):
                rows = slice(w * BLOCK, (w + 1) * BLOCK)
                s = s_ref[slot, rows, lanes]
                if w == blocks - 1:
                    s = s + tri
                ex = jnp.exp2((s - m) * cexp)
                s_ref[slot, rows, lanes] = ex
                et = ex * t_ref[slot, rows, lanes]
                u = u_ref[slot, rows, lanes]
                z8 = z8 + jnp.sum(fold(ex), axis=0)
                et8 = et8 + jnp.sum(fold(et), axis=0)
                eu8 = eu8 + jnp.sum(fold(ex * u), axis=0)
                etu8 = etu8 + jnp.sum(fold(et * u), axis=0)
            inv = 1.0 / jnp.sum(z8, axis=0, keepdims=True)
            mt = jnp.sum(et8, axis=0, keepdims=True) * inv
            mu = jnp.sum(eu8, axis=0, keepdims=True) * inv
            cov = jnp.sum(etu8, axis=0, keepdims=True) * inv - mt * mu
            for w in range(blocks):
                rows = slice(w * BLOCK, (w + 1) * BLOCK)
                coef = s_ref[slot, rows, lanes] * (
                    (t_ref[slot, rows, lanes] - mt) * (u_ref[slot, rows, lanes] - mu) - cov
                )
                c_ref[slot, rows, lanes] = coef.astype(BF16)
            if ahead:
                ahead.pop(0)()
            scales.append(inv * (1.0 / HEAD_DIM))
        return scales

    def gather(n, scales):
        g, b, pair = steps[n]
        slot = n % 3
        win = slice(0, KEYS - (1 - b) * BLOCK)
        hv = dot(keys_t[g, :, win], c_ref[slot, win, :])
        ab = at[:, b * BLOCK : (b + 1) * BLOCK]
        for e in range(2):
            lanes = slice(e * BLOCK, (e + 1) * BLOCK)
            head = (hv[:, lanes] * scales[e]).astype(BF16)
            left = g * ROW + (pair * 2 + e) * HEAD_DIM
            cols = slice(left, left + HEAD_DIM)
            part = dot(ab, head, NT)
            if b == 0:
                out[:, cols] = part
            else:
                out[:, cols] += part

    for matmul in scores(0):
        matmul()
    for n in range(8):
        gather(n, weigh(n, scores(n + 1) if n < 7 else []))
    h = jnp.concatenate([out[:, g * ROW : g * ROW + GFEAT] for g in range(GROUPS)], axis=1)
    lane = lax.broadcasted_iota(jnp.int32, (RANK, 128), 1)
    tail = jnp.zeros((RANK, 128), F32)
    share = 1.0 / (RANK * GROUPS)
    for k, term in enumerate((h * d, h * r, r * r * share, d * d * share, r * d * share)):
        tail = jnp.where(lane == k, jnp.sum(term, keepdims=True), tail)
    for g in range(GROUPS):
        out[:, g * ROW + GFEAT : (g + 1) * ROW] = tail


def prepare(core, qg, chunks, up, dmat):
    vm = pltpu.VMEM
    shapes = [
        (CHUNK, HALF), (CHUNK, HALF), (RANK, CHUNK), (2, BLOCK, BLOCK),
        (GROUPS, SPAN * CHUNK, 2 * HEAD_DIM), (GROUPS, HEAD_DIM, SPAN * CHUNK), (GROUPS, SPAN * CHUNK, HEAD_DIM),
    ]
    return pl.pallas_call(
        prepare_kernel,
        out_shape=[jax.ShapeDtypeStruct(shape, BF16) for shape in shapes],
        in_specs=[pl.BlockSpec(memory_space=pltpu.SMEM)] + [pl.BlockSpec(memory_space=vm)] * 6,
        out_specs=[pl.BlockSpec(memory_space=vm)] * len(shapes),
        compiler_params=pltpu.CompilerParams(vmem_limit_bytes=24 * 1024 * 1024),
        name="prepare",
    )(core, qg, *chunks, up, dmat)


def attend(core, qg, far, ready, dmat, rmat):
    vm = pltpu.VMEM
    return pl.pallas_call(
        attend_kernel,
        out_shape=jax.ShapeDtypeStruct((RANK, GROUPS * ROW), F32),
        in_specs=[pl.BlockSpec(memory_space=x) for x in (pltpu.SMEM, vm, pl.ANY) + (vm,) * 9],
        out_specs=pl.BlockSpec(memory_space=vm),
        scratch_shapes=[
            vm((2, BLOCK + SEG_ROWS, 4 * KHALF), BF16),
            pltpu.SemaphoreType.DMA,
            vm((GROUPS, KEYS, 2 * HEAD_DIM), BF16),
            vm((GROUPS, HEAD_DIM, KEYS), BF16),
            vm((GROUPS, KEYS, HEAD_DIM), BF16),
            vm((3, KEYS, CHUNK), F32),
            vm((3, KEYS, CHUNK), F32),
            vm((3, KEYS, CHUNK), F32),
            vm((3, KEYS, CHUNK), BF16),
        ],
        compiler_params=pltpu.CompilerParams(vmem_limit_bytes=40 * 1024 * 1024),
        cost_estimate=pl.CostEstimate(flops=2_000_000_000, bytes_accessed=4_000_000, transcendentals=2_000_000),
        name="attend",
    )(core, qg, far, *ready, dmat, rmat)


def norm_kernel(got, h_out, out):
    total = jnp.sum(got[...], axis=0)
    h = total[:, : h_out.shape[1]]
    h_out[...] = h
    tail = total[:, h_out.shape[1] :]
    lane = lax.broadcasted_iota(jnp.int32, tail.shape, 1)
    share = 2.0 / out.shape[0]
    row = jnp.where(lane == 5, jnp.sum(h * h, keepdims=True), tail * share)
    out[...] = jnp.broadcast_to(row[None], out.shape)


def update_kernel(damping, got, h_all, parts, new_solution, new_residual, new_direction, spread):
    total = jnp.sum(got[...], axis=0)
    lane = lax.broadcasted_iota(jnp.int32, total.shape, 1)

    def pick(row, k):
        return jnp.sum(jnp.where(lane == k, row, 0.0), keepdims=True)

    dh, rh, rr, dd, rd, hh = (pick(total, k) for k in range(6))
    damp = damping[0]
    h = h_all[...]
    sol, res, dirn = parts[0:1], parts[1:2], parts[2:3]
    step_len = rr / (dd + dh / damp)
    curved = dirn + h / damp
    rc = rd + rh / damp
    cc = dd + 2.0 * dh / damp + hh / (damp * damp)
    new_norm = rr - 2.0 * step_len * rc + step_len * step_len * cc
    ns = sol + step_len * dirn
    nr = res - step_len * curved
    new_solution[...] = ns
    new_residual[...] = nr
    new_direction[...] = nr + (new_norm / rr) * dirn
    spread[...] = jnp.broadcast_to(ns[None], spread.shape)


def in_vmem(kernel, out_shapes, *args, name, dtype=F32, smem=0):
    return pl.pallas_call(
        kernel,
        out_shape=[jax.ShapeDtypeStruct(s, dtype) for s in out_shapes],
        in_specs=[pl.BlockSpec(memory_space=pltpu.SMEM if i < smem else pltpu.VMEM) for i in range(len(args))],
        out_specs=[pl.BlockSpec(memory_space=pltpu.VMEM)] * len(out_shapes),
        name=name,
    )(*args)


def exchange(x, axes):
    return lax.all_to_all(x, axes, 0, 0, tiled=True)


def spot(yh, z, core, n_z):
    return (yh * n_z + z) * 2 + core


def moves(n_yh, n_z, kinds):
    pairs = []
    for source, target, up in kinds:
        for yh in range(n_yh - up):
            for core in range(2):
                pairs.append((spot(yh, source, core, n_z), spot(yh + up, target, core, n_z)))
    return pairs


def per_device(
    base_queries, adapter_input, adapter_up_weight, projected_keys, projected_values, output_gradient,
    segments, solution, residual, direction, damping,
):
    core, z = lax.axis_index("core"), lax.axis_index("z")
    n_yh, n_z, n_task = lax.axis_size("yh"), lax.axis_size("z"), lax.axis_size("task")
    idx = lax.axis_index(CTX)

    last = n_z - 1
    row = [(i, i + 1, 0) for i in range(last)]

    def move(x, *kinds):
        return lax.ppermute(x, CTX, moves(n_yh, n_z, kinds))

    (own,) = in_vmem(
        pack_kernel, [(BLOCK + SEG_ROWS, 4 * KHALF)], projected_keys[0], projected_values[0], segments, name="pack", dtype=BF16
    )
    (qg,) = in_vmem(
        pack_queries_kernel, [(2, BLOCK, 2 * HALF + 128)], base_queries[0], output_gradient[0], adapter_input[0].T,
        name="pack_queries", dtype=BF16,
    )
    cross = move(own, (last, 1, 1), (last - 1, 0, 1), (last - 2, 2, 1))
    first = move(own, *row)
    qg = exchange(qg, "core").reshape(CHUNK, 2 * HALF + 128)
    own = lax.all_gather(own, "core")
    up, dmat, rmat = (x.reshape(RANK, 2 * HALF) for x in (adapter_up_weight, direction, residual))
    size = direction.shape[1] // (n_yh * n_z * 2)
    parts = jnp.concatenate([lax.dynamic_slice_in_dim(x, idx * size, size, 1) for x in (solution, residual, direction)])
    first, qg = lax.optimization_barrier((first, qg))
    second = move(first, *row[1:])
    cross, own, dmat, rmat, parts = lax.optimization_barrier((cross, own, dmat, rmat, parts))
    second = jnp.where(z <= 1, cross, second)
    back = move(cross, (1, 0, 0))
    far = move(cross, (2, 0, 0))
    third = move(second, *row)
    second = lax.all_gather(second, "core")
    second, far, first = lax.optimization_barrier((second, far, first))
    first = lax.all_gather(jnp.where(z == 0, far, first), "core")
    ready = prepare(core.reshape(1), qg, (second, first, own), up, dmat)
    back, third, *ready = lax.optimization_barrier((back, third, *ready))
    late = lax.all_gather(jnp.where(z == 0, back, third), "core")

    terms = attend(core.reshape(1), qg, late, ready, dmat, rmat)

    peers = n_yh * n_z
    h, scalars = in_vmem(
        norm_kernel, [(1, GFEAT), (2 * peers, 1, 128)], exchange(terms.reshape(peers, 1, ROW), ("yh", "z")), name="norm"
    )
    new_solution, new_residual, new_direction, spread = in_vmem(
        update_kernel, [(1, size)] * 3 + [(n_task, 1, size)], damping, exchange(scalars, CTX), h, parts, name="update", smem=1
    )
    meta_gradient = jnp.sum(exchange(spread, "task"), axis=(0, 1)) / n_task
    return new_solution, new_residual, new_direction, meta_gradient


def solution(mesh):
    n_task, n_ctx = mesh.devices.shape
    split = Mesh(mesh.devices.reshape(n_task, n_ctx // 16, 8, 2), ("task",) + CTX)
    tokens = P("task", CTX, None)
    whole = P("task", None)
    in_specs = (tokens, tokens, P("task", None, None), tokens, tokens, tokens, P("task", CTX), whole, whole, whole, P("task"))
    out_specs = (P("task", CTX), P("task", CTX), P("task", CTX), P(CTX))
    return jax.shard_map(per_device, mesh=split, in_specs=in_specs, out_specs=out_specs, check_vma=False)
```
